512 devices in a mesh: pipe: 64 (over y, x, z_lo), head: 8 (over z_hi, core).
Axes of the slice: x: 4, y: 8, z: 8 (z_hi: 4, z_lo: 2; z = z_hi * 2 + z_lo), core: 2. Of those that a mesh axis runs over, the one named last changes fastest.
Arguments:
- stream: bfloat16 [64, 2048, 128], P('pipe', 'head'), may hold values from -6 to 6
- fresh: bfloat16 [2, 2048, 128], P(None, 'head'), may hold values from -6 to 6
- gain: float32 [64, 2048], P('pipe'), may hold values from 0.25 to 1.75
- final_gain: float32 [2048], replicated, may hold values from 0.25 to 1.75
- w_query: bfloat16 [64, 2048, 2048], P('pipe', None, 'head'), may hold values from -0.125 to 0.125
- w_kv: bfloat16 [64, 2, 2048, 2048], P('pipe', None, None, 'head'), may hold values from -0.125 to 0.125
- w_out: bfloat16 [64, 2048, 2048], P('pipe', 'head'), may hold values from -0.125 to 0.125
- cache_kv: bfloat16 [64, 2, 128, 4096], P('pipe', None, None, 'head'), may hold values from -6 to 6
- cache_grad: bfloat16 [64, 128, 4096], P('pipe', None, 'head'), may hold values from -6 to 6
Outputs:
- stream_out: bfloat16 [64, 2048, 128], P('pipe', 'head')
- new_kv: bfloat16 [64, 2, 128, 4096], P('pipe', None, None, 'head')
- memory_grad: float32 [2048, 128], P(('pipe', 'head'))
The draws below stay inside these ranges and needn't reach their ends.
All inputs are finite; a program needn't handle non-finite values.
Results may differ from the reference program's by a relative error of at most 0.017.
Values may be sent and summed in bfloat16 or wider, within the bound.
No kernel may reach another device: no remote copies, remote signals or barrier semaphores. Data moves between devices by JAX's collectives and lax.ppermute only.
A program may use at most 64 MiB of HBM per device.

```python
import jax
import jax.numpy as jnp
from jax import lax

D = 2048
DH = 256
SEQ = 128
TICKS = 2
HEADS = 8
HD = 2048
SECTIONS = 64


def levels(rng, extent, shards, least, largest):
    def one(dim, blocks):
        heights = jax.random.uniform(jax.random.fold_in(jax.random.fold_in(rng, 6), dim), (blocks,), jnp.float32, least / len(shards), largest / len(shards))
        return jnp.repeat(jnp.exp(heights), extent[dim] // blocks).reshape((-1,) + (1,) * (len(extent) - dim - 1))

    level = one(*shards[0])
    for cut in shards[1:]:
        level = level * one(*cut)
    return level


def scatter_about(key, shape, deviation, reach, shards=(), held_as=jnp.bfloat16):
    array = jax.random.normal(key, shape, jnp.float32) * deviation
    if len(shards) > 0:
        array = levels(key, shape, shards, -0.22, 0.18) * array
    return jnp.clip(array, min=-reach, max=reach).astype(held_as)


def setup_inputs(seed: int = 0) -> dict:
    streams_of = jax.random.split(jax.random.key(seed), 10)
    return {
        "stream": scatter_about(streams_of[0], (SECTIONS, D, SEQ), 1.0, 6.0, ((0, 64), (1, 8))),
        "fresh": scatter_about(streams_of[1], (2, D, SEQ), 1.0, 6.0, ((1, 8),)),
        "gain": jnp.clip(1.0 + 0.15 * jax.random.normal(streams_of[2], (SECTIONS, D), jnp.float32), 0.25, 1.75),
        "final_gain": jnp.clip(1.0 + 0.15 * jax.random.normal(streams_of[3], (D,), jnp.float32), 0.25, 1.75),
        "w_query": scatter_about(streams_of[4], (SECTIONS, D, HD), D ** -0.5, 0.125, ((0, 64), (2, 8))),
        "w_kv": scatter_about(streams_of[5], (SECTIONS, 2, D, HD), D ** -0.5, 0.125, ((0, 64), (3, 8))),
        "w_out": scatter_about(streams_of[6], (SECTIONS, HD, D), HD ** -0.5, 0.125, ((0, 64), (1, 8))),
        "cache_kv": scatter_about(streams_of[7], (SECTIONS, TICKS, SEQ, 2 * HD), 1.0, 6.0, ((0, 64), (3, 8))),
        "cache_grad": scatter_about(streams_of[8], (SECTIONS, SEQ, 2 * HD), 1.0, 6.0, ((0, 64), (2, 8))),
    }


EPS = 1e-06

def rms_norm(values, scale_row):
    wide = values.astype(jnp.float32)
    factor = lax.rsqrt(lax.optimization_barrier(jnp.mean(wide * wide, axis=-1, keepdims=True)) + EPS)
    return (wide * factor * scale_row.astype(jnp.float32)).astype(jnp.bfloat16)

def kv_join(keys, values):
    rows = keys.shape[0]
    both = jnp.stack([keys.reshape(rows, HEADS, DH), values.reshape(rows, HEADS, DH)], axis=2)
    return both.reshape(rows, 2 * HD)

def kv_part(joined):
    rows = joined.shape[0]
    both = joined.reshape(rows, HEADS, 2, DH)
    return (both[:, :, 0, :], both[:, :, 1, :])

def section_forward(args):
    columns, scale_row, wq, wkv, wo, cross, is_enc = args
    inputs = columns.T
    normed = rms_norm(inputs, scale_row)
    query = jnp.dot(normed, wq, preferred_element_type=jnp.float32).astype(jnp.bfloat16)
    rows = inputs.shape[0]

    def own():
        keys = jnp.dot(normed, wkv[0], preferred_element_type=jnp.float32).astype(jnp.bfloat16)
        values = jnp.dot(normed, wkv[1], preferred_element_type=jnp.float32).astype(jnp.bfloat16)
        return (keys.reshape(rows, HEADS, DH), values.reshape(rows, HEADS, DH))

    def other():
        return kv_part(cross)
    keys, values = lax.cond(is_enc, own, other)
    heads_q = query.reshape(rows, HEADS, DH).astype(jnp.float32)
    scores = jnp.einsum('qhd,khd->hqk', heads_q, keys.astype(jnp.float32)) * DH ** (-0.5)
    probs = jax.nn.softmax(scores, axis=-1).astype(jnp.bfloat16)
    attn = jnp.einsum('hqk,khd->qhd', probs.astype(jnp.float32), values.astype(jnp.float32)).astype(jnp.bfloat16)
    wo_heads = wo.reshape(HEADS, DH, D).astype(jnp.float32)
    partial_value = jnp.einsum('qhd,hde->hqe', attn.astype(jnp.float32), wo_heads).astype(jnp.bfloat16)
    summed = lax.optimization_barrier(jnp.sum(partial_value.astype(jnp.float32), axis=0))
    return (inputs.astype(jnp.float32) + summed).astype(jnp.bfloat16).T

def reference(stream, fresh, gain, final_gain, w_query, w_kv, w_out, cache_kv, cache_grad):
    half = SECTIONS // 2
    sections = jnp.arange(SECTIONS)
    decoder = (sections >= half)[:, None, None]
    current = stream
    produced = []
    previous = None
    for tick in range(TICKS):
        cross = cache_kv[:, tick]
        if tick > 0:
            cross = cross.at[half].set(previous[half])
        outputs = lax.map(section_forward, (current, gain, w_query, w_kv, w_out, cross, sections < half))
        memory = rms_norm(outputs[half - 1].T, final_gain)

        def cross_of(wkv):
            keys = jnp.dot(memory, wkv[0], preferred_element_type=jnp.float32).astype(jnp.bfloat16)
            values = jnp.dot(memory, wkv[1], preferred_element_type=jnp.float32).astype(jnp.bfloat16)
            return kv_join(keys, values)
        made = lax.map(cross_of, w_kv)
        made = jnp.where(decoder, made, jnp.zeros_like(made))
        produced.append(made)
        previous = made
        shifted = jnp.concatenate([jnp.zeros_like(outputs[:1]), outputs[:-1]], axis=0)
        if tick + 1 < TICKS:
            shifted = shifted.at[0].set(fresh[0]).at[half].set(fresh[1])
        else:
            shifted = shifted.at[half].set(jnp.zeros_like(fresh[1]))
        current = shifted

    def add_section(total, pair):
        wkv, grads = pair
        grad_keys, grad_values = kv_part(grads)
        rows = grads.shape[0]
        term = jnp.dot(wkv[0], grad_keys.reshape(rows, HD).T, preferred_element_type=jnp.float32)
        term = term + jnp.dot(wkv[1], grad_values.reshape(rows, HD).T, preferred_element_type=jnp.float32)
        return (total + term, None)
    start_total = jnp.zeros((D, SEQ), jnp.float32)
    memory_grad, _ = lax.scan(add_section, start_total, (w_kv[half:], cache_grad[half:]))
    return (current, jnp.stack(produced, axis=1), memory_grad)
```

```python
import jax
import jax.numpy as jnp
from jax import lax
from jax.experimental import pallas as pl
from jax.experimental.pallas import tpu as pltpu
from jax.sharding import Mesh, PartitionSpec as P

TICKS = 2
EPS = 1e-06
PIPE = ("y", "x", "zl")
HEAD = ("zh", "c")
Y, X, ZL, ZH, C = 8, 4, 2, 4, 2
BF, F32 = jnp.bfloat16, jnp.float32


def place(y, x, zl):
    return (y * X + x) * ZL + zl


def norm_into(out, source, scale):
    heads, tokens, width = source.shape
    total = jnp.zeros((tokens, width), F32)
    for h in range(heads):
        wide = source[h].astype(F32)
        total = total + wide * wide
    mean = jnp.sum(total, axis=1, keepdims=True) / (heads * width)
    factor = lax.rsqrt(mean + EPS)
    for h in range(heads):
        wide = source[h].astype(F32)
        out[h] = (wide * factor * scale[h]).astype(BF)


def project(rows, weight):
    heads, tokens, width = rows.shape
    total = jnp.zeros((tokens, weight.shape[1]), F32)
    for h in range(heads):
        total = total + jnp.dot(
            rows[h], weight[h * width : (h + 1) * width, :], preferred_element_type=F32
        )
    return total.astype(BF)


def attend_and_project(query, pair, wo, out):
    width = query.shape[1]
    scores = lax.dot_general(
        query, pair[:, :width], (((1,), (1,)), ((), ())), preferred_element_type=F32
    )
    scores = scores * width ** (-0.5)
    scores = jnp.exp(scores - jnp.max(scores, axis=-1, keepdims=True))
    probs = (scores / jnp.sum(scores, axis=-1, keepdims=True)).astype(BF)
    attn = jnp.dot(probs, pair[:, width:], preferred_element_type=F32).astype(BF)
    for h in range(out.shape[0]):
        out[h] = jnp.dot(
            attn, wo[:, h * width : (h + 1) * width], preferred_element_type=F32
        ).astype(BF)


def first_kernel(section, half, x, gain, wq, wkv, wo, cross, out, normed, pair):
    width = wq.shape[1]
    norm_into(normed, x, gain)
    query = project(normed, wq)

    @pl.when(section[0] < half)
    def _():
        pair[:, :width] = project(normed, wkv.at[0])
        pair[:, width:] = project(normed, wkv.at[1])

    @pl.when(section[0] >= half)
    def _():
        pair[...] = cross[...]

    attend_and_project(query, pair, wo, out)


def second_kernel(
    section, half, x, fresh, gain, final_gain, wq, wkv, wo, cross, out, normed, kv_rows, pair
):
    width = wq.shape[1]

    @pl.when(section[0] == half)
    def _():
        norm_into(normed, fresh, gain)
        norm_into(kv_rows, x, final_gain)
        pair[:, :width] = project(kv_rows, wkv.at[0])
        pair[:, width:] = project(kv_rows, wkv.at[1])

    @pl.when(section[0] != half)
    def _():
        norm_into(normed, x, gain)

    @pl.when(section[0] < half)
    def _():
        pair[:, :width] = project(normed, wkv.at[0])
        pair[:, width:] = project(normed, wkv.at[1])

    @pl.when(section[0] > half)
    def _():
        pair[...] = cross[...]

    attend_and_project(project(normed, wq), pair, wo, out)


def memory_kernel(section, half, first, second, final_gain, wkv, out, rows):
    width = wkv.shape[2]

    @pl.when(section[0] >= half)
    def _():
        for t, source in enumerate((first, second)):
            norm_into(rows, source, final_gain)
            out[t, :, :width] = project(rows, wkv.at[0])
            out[t, :, width:] = project(rows, wkv.at[1])

    @pl.when(section[0] < half)
    def _():
        out[...] = jnp.zeros_like(out)


def call(kernel, section, half, operands, out_shape, scratch, cost):
    def with_half(section_ref, *refs):
        kernel(section_ref, half, *refs)

    return pl.pallas_call(
        with_half,
        out_shape=jax.ShapeDtypeStruct(out_shape, BF),
        in_specs=[pl.BlockSpec(memory_space=pltpu.SMEM)]
        + [pl.BlockSpec(memory_space=pltpu.VMEM)] * len(operands),
        out_specs=pl.BlockSpec(memory_space=pltpu.VMEM),
        scratch_shapes=[pltpu.VMEM(shape, BF) for shape in scratch],
        compiler_params=pltpu.CompilerParams(vmem_limit_bytes=24 * 1024 * 1024),
        cost_estimate=pl.CostEstimate(flops=cost, bytes_accessed=5_000_000, transcendentals=0),
    )(section, *operands)


def spread(block, source):
    y, x, zl = lax.axis_index("y"), lax.axis_index("x"), lax.axis_index("zl")
    sy, sx, sz = source // (X * ZL), source // ZL % X, source % ZL
    held = block
    for to in range(sy + 1, Y):
        sent = lax.ppermute(block, PIPE, [(source, place(to, sx, sz))])
        held = jnp.where(y == to, sent, held)
    column = held
    for to in range(X):
        if to != sx:
            pairs = [(place(k, sx, sz), place(k, to, sz)) for k in range(sy + 1, Y)]
            held = jnp.where(x == to, lax.ppermute(column, PIPE, pairs), held)
    pairs = [
        (place(k, to, sz), place(k, to, 1 - sz)) for k in range(sy + 1, Y) for to in range(X)
    ]
    return jnp.where(zl == sz, held, lax.ppermute(held, PIPE, pairs))


def body(stream, fresh, gain, final_gain, w_query, w_kv, w_out, cache_kv, cache_grad):
    pipe_count, heads = Y * X * ZL, ZH * C
    half = pipe_count // 2
    place_here = lax.axis_index(PIPE)
    section = place_here.astype(jnp.int32)[None]
    wq, wkv, wo = w_query[0], w_kv[0], w_out[0]
    depth, width = wq.shape
    tokens = stream.shape[2]
    scale = gain[0].reshape(heads, 1, width)
    final_scale = final_gain.reshape(heads, 1, width)

    grads = jnp.where(place_here >= half, cache_grad[0], jnp.zeros_like(cache_grad[0]))
    rows_by = (((1,), (1,)), ((), ()))
    share = lax.dot_general(wkv[0], grads[:, :width], rows_by, preferred_element_type=F32)
    share = share + lax.dot_general(wkv[1], grads[:, width:], rows_by, preferred_element_type=F32)
    share = lax.psum_scatter(share, "y", scatter_dimension=0, tiled=True)
    share = lax.psum_scatter(share, "x", scatter_dimension=0, tiled=True)
    share = share.reshape(ZL * heads, 1, depth // (pipe_count * heads), tokens)
    share = jnp.concatenate([share, share, share, share], axis=1)
    share = lax.psum_scatter(share, ("zl",) + HEAD, scatter_dimension=0, tiled=False)
    memory_grad = share[0]

    def whole(block):
        return lax.all_gather(block, HEAD, axis=0)

    def summed(parts, current):
        parts = lax.all_to_all(parts, HEAD, 0, 0, tiled=True)
        return (current.astype(F32) + jnp.sum(parts.astype(F32), axis=0)).astype(BF)

    shift = [(i, i + 1) for i in range(pipe_count - 1)]
    fresh_rows = jnp.swapaxes(fresh, 1, 2)
    fresh_whole = lax.all_gather(fresh_rows, HEAD, axis=0)[:, 1]

    rows8 = (heads, tokens, width)
    pair_shape = (tokens, 2 * width)
    flops = 2 * tokens * depth * width * 4

    current = stream[0].T
    parts = call(
        first_kernel, section, half,
        (whole(current), scale, wq, wkv, wo, cache_kv[0, 0]),
        rows8, (rows8, pair_shape), flops,
    )
    output = summed(parts, current)
    passed = lax.ppermute(output, PIPE, shift)
    first_memory = spread(output, half - 1)

    current = jnp.where(place_here == 0, fresh_rows[0], passed)
    parts = call(
        second_kernel, section, half,
        (whole(current), fresh_whole, scale, final_scale, wq, wkv, wo, cache_kv[0, 1]),
        rows8, (rows8, rows8, pair_shape), flops,
    )
    current = jnp.where(place_here == half, fresh_rows[1], current)
    output = summed(parts, current)
    passed = lax.ppermute(output, PIPE, shift)
    last = jnp.where(place_here == half, jnp.zeros_like(passed), passed)

    second_memory = spread(output, half - 1)
    new_kv = call(
        memory_kernel, section, half,
        (whole(first_memory), whole(second_memory), final_scale, wkv),
        (TICKS, tokens, 2 * width), (rows8,), flops,
    )
    return (last.T[None], new_kv[None], memory_grad)


def solution(mesh):
    split = Mesh(mesh.devices.reshape(Y, X, ZL, ZH, C), PIPE + HEAD)
    return jax.shard_map(
        body,
        mesh=split,
        in_specs=(
            P(PIPE, HEAD, None),
            P(None, HEAD, None),
            P(PIPE, None),
            P(),
            P(PIPE, None, HEAD),
            P(PIPE, None, None, HEAD),
            P(PIPE, HEAD, None),
            P(PIPE, None, None, HEAD),
            P(PIPE, None, HEAD),
        ),
        out_specs=(
            P(PIPE, HEAD, None),
            P(PIPE, None, None, HEAD),
            P(PIPE + HEAD, None),
        ),
        check_vma=False,
    )
```

```python
import functools

import jax
import jax.numpy as jnp
from jax import lax
from jax.experimental import pallas as pl
from jax.experimental.pallas import tpu as pltpu
from jax.sharding import Mesh, PartitionSpec as P

TICKS = 2
EPS = 1e-06
PIPE = ("y", "x", "zl")
HEAD = ("zh", "c")
Y, X, ZL, ZH, C = 8, 4, 2, 4, 2
BF, F32 = jnp.bfloat16, jnp.float32


def place(y, x, zl):
    return (y * X + x) * ZL + zl


def norm_into(out, source, scale):
    heads, tokens, width = source.shape
    total = jnp.zeros((tokens, width), F32)
    for h in range(heads):
        wide = source[h].astype(F32)
        total = total + wide * wide
    mean = jnp.sum(total, axis=1, keepdims=True) / (heads * width)
    factor = lax.rsqrt(mean + EPS)
    for h in range(heads):
        wide = source[h].astype(F32)
        out[h] = (wide * factor * scale[:, h * width : (h + 1) * width]).astype(BF)


def project(rows, weight):
    heads, tokens, width = rows.shape
    total = jnp.zeros((tokens, weight.shape[1]), F32)
    for h in range(heads):
        total = total + jnp.dot(
            rows[h], weight[h * width : (h + 1) * width, :], preferred_element_type=F32
        )
    return total.astype(BF)


def attend(query, pair):
    width = query.shape[1]
    scores = lax.dot_general(
        query, pair[:, :width], (((1,), (1,)), ((), ())), preferred_element_type=F32
    )
    scores = scores * width ** (-0.5)
    scores = jnp.exp(scores - jnp.max(scores, axis=-1, keepdims=True))
    probs = (scores / jnp.sum(scores, axis=-1, keepdims=True)).astype(BF)
    return jnp.dot(probs, pair[:, width:], preferred_element_type=F32).astype(BF)


def tick_kernel(tick, half, section, x_hbm, fresh_hbm, gain_hbm, final_hbm, wq_hbm, wkv_hbm, wo_hbm,
                cache_hbm, out_hbm, x, fresh, fresh_rows, gain, final_gain, wq, wkv, wo, pair, normed,
                kv_rows, out, sems):
    heads, tokens, width = x.shape
    here = section[0]
    in_encoder = here < half
    at_half = here == half if tick > 0 else here < 0
    own_pair = jnp.logical_or(in_encoder, at_half)

    def copy(k, source, target):
        return pltpu.make_async_copy(source, target, sems.at[k])

    get_x = copy(0, x_hbm, x)
    get_gain = copy(1, gain_hbm, gain)
    get_wq = copy(2, wq_hbm.at[0], wq)
    get_wkv = copy(3, wkv_hbm.at[0], wkv)
    get_cache = copy(4, cache_hbm.at[0, tick], pair)
    get_wo = copy(5, wo_hbm.at[0], wo)
    get_x.start()
    get_gain.start()
    get_wq.start()
    pl.when(own_pair)(get_wkv.start)
    pl.when(jnp.logical_not(own_pair))(get_cache.start)
    get_wo.start()
    get_x.wait()
    get_gain.wait()
    if tick == 0:
        norm_into(normed, x, gain)
    else:
        get_fresh = copy(6, fresh_hbm.at[:, 1], fresh)
        get_final = copy(7, final_hbm, final_gain)

        @pl.when(at_half)
        def _():
            get_fresh.start()
            get_final.start()
            get_fresh.wait()
            get_final.wait()
            for h in range(heads):
                fresh_rows[h] = fresh[h].T
            norm_into(normed, fresh_rows, gain)
            norm_into(kv_rows, x, final_gain)

        @pl.when(jnp.logical_not(at_half))
        def _():
            norm_into(normed, x, gain)

    get_wq.wait()
    query = project(normed, wq)

    @pl.when(in_encoder)
    def _():
        get_wkv.wait()
        pair[:, :width] = project(normed, wkv.at[0])
        pair[:, width:] = project(normed, wkv.at[1])

    if tick > 0:

        @pl.when(at_half)
        def _():
            get_wkv.wait()
            pair[:, :width] = project(kv_rows, wkv.at[0])
            pair[:, width:] = project(kv_rows, wkv.at[1])

    @pl.when(jnp.logical_not(own_pair))
    def _():
        get_cache.wait()

    attn = attend(query, pair)
    get_wo.wait()
    puts = []
    for h in range(heads):
        out[h] = jnp.dot(
            attn, wo[:, h * width : (h + 1) * width], preferred_element_type=F32
        ).astype(BF)
        puts.append(copy(8 + h, out.at[h], out_hbm.at[h]))
        puts[-1].start()
    for put in puts:
        put.wait()


def memory_kernel(half, section, first_hbm, second_hbm, final_hbm, wkv_hbm, out_hbm, sources, rows,
                  final_gain, wkv, out, sems):
    width = wkv.shape[2]

    def copy(k, source, target):
        return pltpu.make_async_copy(source, target, sems.at[k])

    gets = [
        copy(0, second_hbm, sources.at[1]),
        copy(1, final_hbm, final_gain),
        copy(2, first_hbm.at[:, 0], sources.at[0]),
        copy(3, wkv_hbm.at[0], wkv),
    ]

    @pl.when(section[0] >= half)
    def _():
        for get in gets:
            get.start()
        for get in gets[:3]:
            get.wait()
        for t in range(TICKS):
            norm_into(rows.at[t], sources.at[t], final_gain)
        gets[3].wait()
        for t in range(TICKS):
            out[t, :, :width] = project(rows.at[t], wkv.at[0])
            out[t, :, width:] = project(rows.at[t], wkv.at[1])

    @pl.when(section[0] < half)
    def _():
        out[...] = jnp.zeros_like(out)

    put = copy(4, out, out_hbm.at[0])
    put.start()
    put.wait()


def call(kernel, section, operands, out_shape, scratch, copies, flops):
    return pl.pallas_call(
        kernel,
        out_shape=jax.ShapeDtypeStruct(out_shape, BF),
        in_specs=[pl.BlockSpec(memory_space=pltpu.SMEM)]
        + [pl.BlockSpec(memory_space=pl.ANY)] * len(operands),
        out_specs=pl.BlockSpec(memory_space=pl.ANY),
        scratch_shapes=[pltpu.VMEM(shape, kind) for shape, kind in scratch]
        + [pltpu.SemaphoreType.DMA((copies,))],
        compiler_params=pltpu.CompilerParams(vmem_limit_bytes=40 * 1024 * 1024),
        cost_estimate=pl.CostEstimate(flops=flops, bytes_accessed=5_000_000, transcendentals=0),
    )(section, *operands)


def spread(block, source):
    y, x, zl = lax.axis_index("y"), lax.axis_index("x"), lax.axis_index("zl")
    sy, sx, sz = source // (X * ZL), source // ZL % X, source % ZL
    held = block
    for to in range(sy + 1, Y):
        sent = lax.ppermute(block, PIPE, [(source, place(to, sx, sz))])
        held = jnp.where(y == to, sent, held)
    column = held
    for to in range(X):
        if to != sx:
            pairs = [(place(k, sx, sz), place(k, to, sz)) for k in range(sy + 1, Y)]
            held = jnp.where(x == to, lax.ppermute(column, PIPE, pairs), held)
    pairs = [
        (place(k, to, sz), place(k, to, 1 - sz)) for k in range(sy + 1, Y) for to in range(X)
    ]
    return jnp.where(zl == sz, held, lax.ppermute(held, PIPE, pairs))


def body(stream, fresh, gain, final_gain, w_query, w_kv, w_out, cache_kv, cache_grad):
    pipe_count, heads = Y * X * ZL, ZH * C
    half = pipe_count // 2
    place_here = lax.axis_index(PIPE)
    section = place_here.astype(jnp.int32)[None]
    wkv = w_kv[0]
    depth, width = wkv.shape[1:]
    tokens = stream.shape[2]
    final_scale = final_gain[None]
    rows8 = (heads, tokens, width)
    columns8 = (heads, width, tokens)
    pair_shape = (tokens, 2 * width)
    flops = 2 * tokens * depth * width * 4
    shift = [(i, i + 1) for i in range(pipe_count - 1)]

    def whole(block):
        return lax.all_gather(block, HEAD, axis=0)

    def summed(parts, current):
        parts = lax.all_to_all(parts, HEAD, 0, 0, tiled=True)
        return (current.astype(F32) + jnp.sum(parts.astype(F32), axis=0)).astype(BF)

    def run_tick(tick, gathered):
        return call(
            functools.partial(tick_kernel, tick, half), section,
            (gathered, fresh_whole, gain, final_scale, w_query, w_kv, w_out, cache_kv), rows8,
            ((rows8, BF), (columns8, BF), (rows8, BF), ((1, depth), F32), ((1, depth), F32),
             ((depth, width), BF), ((2, depth, width), BF), ((width, depth), BF),
             (pair_shape, BF), (rows8, BF), (rows8, BF), (rows8, BF)),
            8 + heads, flops,
        )

    fresh_whole = whole(fresh)
    current = stream[0].T
    parts = run_tick(0, whole(current))

    grads, fresh_blocks, parts = lax.optimization_barrier((cache_grad[0], fresh, parts))
    grads = jnp.where(place_here >= half, grads, jnp.zeros_like(grads))
    rows_by = (((1,), (1,)), ((), ()))
    share = lax.dot_general(wkv[0], grads[:, :width], rows_by, preferred_element_type=F32)
    share = share + lax.dot_general(wkv[1], grads[:, width:], rows_by, preferred_element_type=F32)
    share = lax.psum_scatter(share, "y", scatter_dimension=0, tiled=True)
    plane = X * ZL * heads
    share = share.reshape(plane, depth // (pipe_count * heads), tokens)
    fresh_rows = jnp.swapaxes(fresh_blocks, 1, 2)

    output = summed(parts, current)
    passed = lax.ppermute(output, PIPE, shift)
    first_memory = spread(output, half - 1)
    entering = output

    current = jnp.where(place_here == 0, fresh_rows[0], passed)
    parts = run_tick(1, whole(current))
    share, parts = lax.optimization_barrier((share, parts))
    share = lax.all_to_all(share, PIPE[1:] + HEAD, 0, 0, tiled=True)
    memory_grad = jnp.sum(share, axis=0)

    current = jnp.where(place_here == half, fresh_rows[1], current)
    output = summed(parts, current)
    output, first_memory = lax.optimization_barrier((output, first_memory))
    second_memory = spread(output, half - 1)
    first_memory = whole(jnp.stack([first_memory, entering]))
    passed = lax.ppermute(output, PIPE, shift)
    last = jnp.where(place_here == half, jnp.zeros_like(passed), passed)

    new_kv = call(
        functools.partial(memory_kernel, half), section,
        (first_memory, whole(second_memory), final_scale, w_kv),
        (1, TICKS, tokens, 2 * width),
        (((TICKS,) + rows8, BF), ((TICKS,) + rows8, BF), ((1, depth), F32),
         ((2, depth, width), BF), ((TICKS,) + pair_shape, BF)),
        5, flops,
    )
    return (last.T[None], new_kv, memory_grad)


def solution(mesh):
    split = Mesh(mesh.devices.reshape(Y, X, ZL, ZH, C), PIPE + HEAD)
    return jax.shard_map(
        body,
        mesh=split,
        in_specs=(
            P(PIPE, HEAD, None),
            P(None, HEAD, None),
            P(PIPE, None),
            P(),
            P(PIPE, None, HEAD),
            P(PIPE, None, None, HEAD),
            P(PIPE, HEAD, None),
            P(PIPE, None, None, HEAD),
            P(PIPE, None, HEAD),
        ),
        out_specs=(
            P(PIPE, HEAD, None),
            P(PIPE, None, None, HEAD),
            P(PIPE + HEAD, None),
        ),
        check_vma=False,
    )
```

```python
import functools

import jax
import jax.numpy as jnp
from jax import lax
from jax.experimental import pallas as pl
from jax.experimental.pallas import tpu as pltpu
from jax.sharding import Mesh, PartitionSpec as P

TICKS = 2
EPS = 1e-06
PIPE = ("y", "x", "zl")
HEAD = ("zh", "c")
Y, X, ZL, ZH, C = 8, 4, 2, 4, 2
BF, F32 = jnp.bfloat16, jnp.float32


def place(y, x, zl):
    return (y * X + x) * ZL + zl


def norm_into(out, source, scale):
    heads, tokens, width = source.shape
    total = jnp.zeros((tokens, width), F32)
    for h in range(heads):
        wide = source[h].astype(F32)
        total = total + wide * wide
    mean = jnp.sum(total, axis=1, keepdims=True) / (heads * width)
    factor = lax.rsqrt(mean + EPS)
    for h in range(heads):
        wide = source[h].astype(F32)
        out[h] = (wide * factor * scale[:, h * width : (h + 1) * width]).astype(BF)


def project(rows, weight):
    heads, tokens, width = rows.shape
    total = jnp.zeros((tokens, weight.shape[1]), F32)
    for h in range(heads):
        total = total + jnp.dot(
            rows[h], weight[h * width : (h + 1) * width, :], preferred_element_type=F32
        )
    return total.astype(BF)


def attend(query, pair):
    width = query.shape[1]
    scores = lax.dot_general(
        query, pair[:, :width], (((1,), (1,)), ((), ())), preferred_element_type=F32
    )
    scores = scores * width ** (-0.5)
    scores = jnp.exp(scores - jnp.max(scores, axis=-1, keepdims=True))
    probs = (scores / jnp.sum(scores, axis=-1, keepdims=True)).astype(BF)
    return jnp.dot(probs, pair[:, width:], preferred_element_type=F32).astype(BF)


def tick_kernel(tick, half, section, x_hbm, fresh_hbm, gain_hbm, final_hbm, wq_hbm, wkv_hbm, wo_hbm,
                cache_hbm, out_hbm, turned_hbm, x, fresh, turned, gain, final_gain, wq, wkv, wo, pair,
                normed, kv_rows, out, sems):
    heads, tokens, width = x.shape
    here = section[0]
    in_encoder = here < half
    at_half = here == half if tick > 0 else here < 0
    own_pair = jnp.logical_or(in_encoder, at_half)

    def copy(k, source, target):
        return pltpu.make_async_copy(source, target, sems.at[k])

    get_x = copy(0, x_hbm, x)
    get_gain = copy(1, gain_hbm, gain)
    get_wq = copy(2, wq_hbm.at[0], wq)
    get_wkv = copy(3, wkv_hbm.at[0], wkv)
    get_cache = copy(4, cache_hbm.at[0, tick], pair)
    get_wo = copy(5, wo_hbm.at[0], wo)
    get_x.start()
    get_gain.start()
    get_wq.start()
    pl.when(own_pair)(get_wkv.start)
    pl.when(jnp.logical_not(own_pair))(get_cache.start)
    get_wo.start()
    if tick == 0:
        get_fresh = copy(6, fresh_hbm, fresh)
        get_fresh.start()
    get_x.wait()
    get_gain.wait()
    if tick == 0:
        norm_into(normed, x, gain)
        get_fresh.wait()
        for h in range(fresh.shape[0]):
            turned[h] = fresh[h].T
        put_turned = copy(7, turned, turned_hbm)
        put_turned.start()
    else:
        get_fresh = copy(6, fresh_hbm.at[:, 1], fresh)
        get_final = copy(7, final_hbm, final_gain)

        @pl.when(at_half)
        def _():
            get_fresh.start()
            get_final.start()
            get_fresh.wait()
            get_final.wait()
            for h in range(heads):
                turned[h] = fresh[h].T
            norm_into(normed, turned, gain)
            norm_into(kv_rows, x, final_gain)

        @pl.when(jnp.logical_not(at_half))
        def _():
            norm_into(normed, x, gain)

    get_wq.wait()
    query = project(normed, wq)

    @pl.when(in_encoder)
    def _():
        get_wkv.wait()
        pair[:, :width] = project(normed, wkv.at[0])
        pair[:, width:] = project(normed, wkv.at[1])

    if tick > 0:

        @pl.when(at_half)
        def _():
            get_wkv.wait()
            pair[:, :width] = project(kv_rows, wkv.at[0])
            pair[:, width:] = project(kv_rows, wkv.at[1])

    @pl.when(jnp.logical_not(own_pair))
    def _():
        get_cache.wait()

    attn = attend(query, pair)
    get_wo.wait()
    puts = []
    for h in range(heads):
        out[h] = jnp.dot(
            attn, wo[:, h * width : (h + 1) * width], preferred_element_type=F32
        ).astype(BF)
        puts.append(copy(8 + h, out.at[h], out_hbm.at[h]))
        puts[-1].start()
    if tick == 0:
        put_turned.wait()
    for put in puts:
        put.wait()


def first_kernel(half, section, x, fresh, gain, wq, wkv, wo, cache, out, turned, *scratch):
    scratch = scratch[:4] + (None,) + scratch[4:9] + (None,) + scratch[9:]
    tick_kernel(0, half, section, x, fresh, gain, None, wq, wkv, wo, cache, out, turned, *scratch)


def second_kernel(half, section, x, fresh, gain, final, wq, wkv, wo, cache, out, *scratch):
    tick_kernel(1, half, section, x, fresh, gain, final, wq, wkv, wo, cache, out, None, *scratch)


def memory_kernel(half, section, first_hbm, second_hbm, final_hbm, wkv_hbm, out_hbm, sources, rows,
                  final_gain, wkv, out, sems):
    width = wkv.shape[2]

    def copy(k, source, target):
        return pltpu.make_async_copy(source, target, sems.at[k])

    gets = [
        copy(0, second_hbm, sources.at[1]),
        copy(1, final_hbm, final_gain),
        copy(2, first_hbm.at[:, 0], sources.at[0]),
        copy(3, wkv_hbm.at[0], wkv),
    ]

    @pl.when(section[0] >= half)
    def _():
        for get in gets:
            get.start()
        for get in gets[:3]:
            get.wait()
        for t in range(TICKS):
            norm_into(rows.at[t], sources.at[t], final_gain)
        gets[3].wait()
        for t in range(TICKS):
            out[t, :, :width] = project(rows.at[t], wkv.at[0])
            out[t, :, width:] = project(rows.at[t], wkv.at[1])

    @pl.when(section[0] < half)
    def _():
        out[...] = jnp.zeros_like(out)

    put = copy(4, out, out_hbm.at[0])
    put.start()
    put.wait()


def call(kernel, section, operands, out_shapes, scratch, copies, flops):
    return pl.pallas_call(
        kernel,
        out_shape=[jax.ShapeDtypeStruct(shape, BF) for shape in out_shapes],
        in_specs=[pl.BlockSpec(memory_space=pltpu.SMEM)]
        + [pl.BlockSpec(memory_space=pl.ANY)] * len(operands),
        out_specs=[pl.BlockSpec(memory_space=pl.ANY)] * len(out_shapes),
        scratch_shapes=[pltpu.VMEM(shape, kind) for shape, kind in scratch]
        + [pltpu.SemaphoreType.DMA((copies,))],
        compiler_params=pltpu.CompilerParams(vmem_limit_bytes=60 * 1024 * 1024),
        cost_estimate=pl.CostEstimate(flops=flops, bytes_accessed=5_000_000, transcendentals=0),
    )(section, *operands)


def spread(block, source):
    y, x, zl = lax.axis_index("y"), lax.axis_index("x"), lax.axis_index("zl")
    sy, sx, sz = source // (X * ZL), source // ZL % X, source % ZL
    held = block
    for to in range(sy + 1, Y):
        sent = lax.ppermute(block, PIPE, [(source, place(to, sx, sz))])
        held = jnp.where(y == to, sent, held)
    column = held
    for to in range(X):
        if to != sx:
            pairs = [(place(k, sx, sz), place(k, to, sz)) for k in range(sy + 1, Y)]
            held = jnp.where(x == to, lax.ppermute(column, PIPE, pairs), held)
    pairs = [
        (place(k, to, sz), place(k, to, 1 - sz)) for k in range(sy + 1, Y) for to in range(X)
    ]
    return jnp.where(zl == sz, held, lax.ppermute(held, PIPE, pairs))


def body(stream, fresh, gain, final_gain, w_query, w_kv, w_out, cache_kv, cache_grad):
    pipe_count, heads = Y * X * ZL, ZH * C
    half = pipe_count // 2
    place_here = lax.axis_index(PIPE)
    section = place_here.astype(jnp.int32)[None]
    wkv = w_kv[0]
    depth, width = wkv.shape[1:]
    tokens = stream.shape[2]
    final_scale = final_gain[None]
    rows8 = (heads, tokens, width)
    columns8 = (heads, width, tokens)
    pair_shape = (tokens, 2 * width)
    flops = 2 * tokens * depth * width * 4
    shift = [(i, i + 1) for i in range(pipe_count - 1)]

    def whole(block):
        return lax.all_gather(block, HEAD, axis=0)

    def exchanged(parts):
        return lax.all_to_all(parts, HEAD, 0, 0, tiled=True)

    def summed(parts, current):
        return (current.astype(F32) + jnp.sum(parts.astype(F32), axis=0)).astype(BF)

    weights = (((depth, width), BF), ((2, depth, width), BF), ((width, depth), BF))
    fresh_whole = whole(fresh)
    current = stream[0].T
    parts, fresh_rows = call(
        functools.partial(first_kernel, half), section,
        (whole(current), fresh, gain, w_query, w_kv, w_out, cache_kv),
        (rows8, (2, tokens, width)),
        ((rows8, BF), ((2, width, tokens), BF), ((2, tokens, width), BF), ((1, depth), F32))
        + weights + ((pair_shape, BF), (rows8, BF), (rows8, BF)),
        8 + heads, flops,
    )

    grads = jnp.where(place_here >= half, cache_grad[0], jnp.zeros_like(cache_grad[0]))
    rows_by = (((1,), (1,)), ((), ()))
    share = lax.dot_general(wkv[0], grads[:, :width], rows_by, preferred_element_type=F32)
    share = share + lax.dot_general(wkv[1], grads[:, width:], rows_by, preferred_element_type=F32)
    share = lax.psum_scatter(share, "y", scatter_dimension=0, tiled=True)
    plane = X * ZL * heads
    share = share.reshape(plane, depth // (pipe_count * heads), tokens)

    output = summed(exchanged(parts), current)
    passed = lax.ppermute(output, PIPE, shift)
    first_memory = spread(output, half - 1)
    entering = output

    current = jnp.where(place_here == 0, fresh_rows[0], passed)
    (parts,) = call(
        functools.partial(second_kernel, half), section,
        (whole(current), fresh_whole, gain, final_scale, w_query, w_kv, w_out, cache_kv),
        (rows8,),
        ((rows8, BF), (columns8, BF), (rows8, BF), ((1, depth), F32), ((1, depth), F32))
        + weights + ((pair_shape, BF), (rows8, BF), (rows8, BF), (rows8, BF)),
        8 + heads, flops,
    )
    share, parts = lax.optimization_barrier((share, parts))
    share = lax.all_to_all(share, PIPE[1:] + HEAD, 0, 0, tiled=True)
    share, parts = lax.optimization_barrier((share, exchanged(parts)))
    memory_grad = jnp.sum(share, axis=0)

    current = jnp.where(place_here == half, fresh_rows[1], current)
    output = summed(parts, current)
    output, first_memory = lax.optimization_barrier((output, first_memory))
    second_memory = spread(output, half - 1)
    first_memory = whole(jnp.stack([first_memory, entering]))
    passed = lax.ppermute(output, PIPE, shift)
    last = jnp.where(place_here == half, jnp.zeros_like(passed), passed)

    (new_kv,) = call(
        functools.partial(memory_kernel, half), section,
        (first_memory, whole(second_memory), final_scale, w_kv),
        ((1, TICKS, tokens, 2 * width),),
        (((TICKS,) + rows8, BF), ((TICKS,) + rows8, BF), ((1, depth), F32),
         ((2, depth, width), BF), ((TICKS,) + pair_shape, BF)),
        5, flops,
    )
    return (last.T[None], new_kv, memory_grad)


def solution(mesh):
    split = Mesh(mesh.devices.reshape(Y, X, ZL, ZH, C), PIPE + HEAD)
    return jax.shard_map(
        body,
        mesh=split,
        in_specs=(
            P(PIPE, HEAD, None),
            P(None, HEAD, None),
            P(PIPE, None),
            P(),
            P(PIPE, None, HEAD),
            P(PIPE, None, None, HEAD),
            P(PIPE, HEAD, None),
            P(PIPE, None, None, HEAD),
            P(PIPE, None, HEAD),
        ),
        out_specs=(
            P(PIPE, HEAD, None),
            P(PIPE, None, None, HEAD),
            P(PIPE + HEAD, None),
        ),
        check_vma=False,
    )
```

```python
import functools

import jax
import jax.numpy as jnp
from jax import lax
from jax.experimental import pallas as pl
from jax.experimental.pallas import tpu as pltpu
from jax.sharding import Mesh, PartitionSpec as P

TICKS = 2
EPS = 1e-06
PIPE = ("y", "x", "zl")
HEAD = ("zh", "c")
Y, X, ZL, ZH, C = 8, 4, 2, 4, 2
BF, F32 = jnp.bfloat16, jnp.float32


def place(y, x, zl):
    return (y * X + x) * ZL + zl


def norm_into(out, source, scale):
    heads, tokens, width = source.shape
    total = jnp.zeros((tokens, width), F32)
    for h in range(heads):
        wide = source[h].astype(F32)
        total = total + wide * wide
    mean = jnp.sum(total, axis=1, keepdims=True) / (heads * width)
    factor = lax.rsqrt(mean + EPS)
    for h in range(heads):
        wide = source[h].astype(F32)
        out[h] = (wide * factor * scale[:, h * width : (h + 1) * width]).astype(BF)


def project(rows, weight):
    heads, tokens, width = rows.shape
    total = jnp.zeros((tokens, weight.shape[1]), F32)
    for h in range(heads):
        total = total + jnp.dot(
            rows[h], weight[h * width : (h + 1) * width, :], preferred_element_type=F32
        )
    return total.astype(BF)


def attend(query, pair):
    width = query.shape[1]
    scores = lax.dot_general(
        query, pair[:, :width], (((1,), (1,)), ((), ())), preferred_element_type=F32
    )
    scores = scores * width ** (-0.5)
    scores = jnp.exp(scores - jnp.max(scores, axis=-1, keepdims=True))
    probs = (scores / jnp.sum(scores, axis=-1, keepdims=True)).astype(BF)
    return jnp.dot(probs, pair[:, width:], preferred_element_type=F32).astype(BF)


def tick_kernel(tick, half, section, x_hbm, fresh_hbm, gain_hbm, final_hbm, wq_hbm, wkv_hbm, wo_hbm,
                cache_hbm, out_hbm, turned_hbm, x, fresh, turned, gain, final_gain, wq, wkv, wo, pair,
                normed, kv_rows, out, sems):
    heads, tokens, width = x.shape
    here = section[0]
    in_encoder = here < half
    at_half = here == half if tick > 0 else here < 0
    own_pair = jnp.logical_or(in_encoder, at_half)

    def copy(k, source, target):
        return pltpu.make_async_copy(source, target, sems.at[k])

    get_x = copy(0, x_hbm, x)
    get_gain = copy(1, gain_hbm, gain)
    get_wq = copy(2, wq_hbm.at[0], wq)
    get_wkv = copy(3, wkv_hbm.at[0], wkv)
    get_cache = copy(4, cache_hbm.at[0, tick], pair)
    get_wo = copy(5, wo_hbm.at[0], wo)
    get_x.start()
    get_gain.start()
    get_wq.start()
    pl.when(own_pair)(get_wkv.start)
    pl.when(jnp.logical_not(own_pair))(get_cache.start)
    get_wo.start()
    if tick == 0:
        get_fresh = copy(6, fresh_hbm, fresh)
        get_fresh.start()
    get_x.wait()
    get_gain.wait()
    if tick == 0:
        norm_into(normed, x, gain)
        get_fresh.wait()
        for h in range(fresh.shape[0]):
            turned[h] = fresh[h].T
        put_turned = copy(7, turned, turned_hbm)
        put_turned.start()
    else:
        get_fresh = copy(6, fresh_hbm.at[:, 1], fresh)
        get_final = copy(7, final_hbm, final_gain)

        @pl.when(at_half)
        def _():
            get_fresh.start()
            get_final.start()
            get_fresh.wait()
            get_final.wait()
            for h in range(heads):
                turned[h] = fresh[h].T
            norm_into(normed, turned, gain)
            norm_into(kv_rows, x, final_gain)

        @pl.when(jnp.logical_not(at_half))
        def _():
            norm_into(normed, x, gain)

    get_wq.wait()
    query = project(normed, wq)

    @pl.when(in_encoder)
    def _():
        get_wkv.wait()
        pair[:, :width] = project(normed, wkv.at[0])
        pair[:, width:] = project(normed, wkv.at[1])

    if tick > 0:

        @pl.when(at_half)
        def _():
            get_wkv.wait()
            pair[:, :width] = project(kv_rows, wkv.at[0])
            pair[:, width:] = project(kv_rows, wkv.at[1])

    @pl.when(jnp.logical_not(own_pair))
    def _():
        get_cache.wait()

    attn = attend(query, pair)
    get_wo.wait()
    puts = []
    for h in range(heads):
        out[h] = jnp.dot(
            attn, wo[:, h * width : (h + 1) * width], preferred_element_type=F32
        ).astype(BF)
        puts.append(copy(8 + h, out.at[h], out_hbm.at[h]))
        puts[-1].start()
    if tick == 0:
        put_turned.wait()
    for put in puts:
        put.wait()


def first_kernel(half, section, x, fresh, gain, wq, wkv, wo, cache, out, turned, *scratch):
    scratch = scratch[:4] + (None,) + scratch[4:9] + (None,) + scratch[9:]
    tick_kernel(0, half, section, x, fresh, gain, None, wq, wkv, wo, cache, out, turned, *scratch)


def second_kernel(half, section, x, fresh, gain, final, wq, wkv, wo, cache, out, *scratch):
    tick_kernel(1, half, section, x, fresh, gain, final, wq, wkv, wo, cache, out, None, *scratch)


def share_kernel(half, section, grads_hbm, wkv_hbm, out_hbm, grads, wkv, total, out, sems):
    width = wkv.shape[2]
    heads, ys, each, xz, _ = out.shape

    @pl.when(section[0] >= half)
    def _():
        get_grads = pltpu.make_async_copy(grads_hbm.at[0], grads, sems.at[0])
        get_wkv = pltpu.make_async_copy(wkv_hbm.at[0], wkv, sems.at[1])
        get_grads.start()
        get_wkv.start()
        get_grads.wait()
        get_wkv.wait()
        rows_by = (((1,), (1,)), ((), ()))
        total[...] = lax.dot_general(
            wkv[0], grads[:, :width], rows_by, preferred_element_type=F32
        ) + lax.dot_general(wkv[1], grads[:, width:], rows_by, preferred_element_type=F32)
        for h in range(heads):
            for y in range(ys):
                for i in range(each):
                    first = y * xz * heads * each + h * each + i
                    out[h, y, i] = total[pl.ds(first, xz, stride=heads * each), :]

    @pl.when(section[0] < half)
    def _():
        out[...] = jnp.zeros_like(out)

    put = pltpu.make_async_copy(out, out_hbm, sems.at[2])
    put.start()
    put.wait()


def memory_kernel(half, section, first_hbm, second_hbm, final_hbm, wkv_hbm, out_hbm, sources, rows,
                  final_gain, wkv, out, sems):
    width = wkv.shape[2]

    def copy(k, source, target):
        return pltpu.make_async_copy(source, target, sems.at[k])

    gets = [
        copy(0, second_hbm, sources.at[1]),
        copy(1, final_hbm, final_gain),
        copy(2, first_hbm.at[:, 0], sources.at[0]),
        copy(3, wkv_hbm.at[0], wkv),
    ]

    @pl.when(section[0] >= half)
    def _():
        for get in gets:
            get.start()
        for get in gets[:3]:
            get.wait()
        for t in range(TICKS):
            norm_into(rows.at[t], sources.at[t], final_gain)
        gets[3].wait()
        for t in range(TICKS):
            out[t, :, :width] = project(rows.at[t], wkv.at[0])
            out[t, :, width:] = project(rows.at[t], wkv.at[1])

    @pl.when(section[0] < half)
    def _():
        out[...] = jnp.zeros_like(out)

    put = copy(4, out, out_hbm.at[0])
    put.start()
    put.wait()


def call(kernel, section, operands, out_shapes, scratch, copies, flops, kind=BF):
    return pl.pallas_call(
        kernel,
        out_shape=[jax.ShapeDtypeStruct(shape, kind) for shape in out_shapes],
        in_specs=[pl.BlockSpec(memory_space=pltpu.SMEM)]
        + [pl.BlockSpec(memory_space=pl.ANY)] * len(operands),
        out_specs=[pl.BlockSpec(memory_space=pl.ANY)] * len(out_shapes),
        scratch_shapes=[pltpu.VMEM(shape, held) for shape, held in scratch]
        + [pltpu.SemaphoreType.DMA((copies,))],
        compiler_params=pltpu.CompilerParams(vmem_limit_bytes=60 * 1024 * 1024),
        cost_estimate=pl.CostEstimate(flops=flops, bytes_accessed=5_000_000, transcendentals=0),
    )(section, *operands)


def spread(block, source):
    y, x, zl = lax.axis_index("y"), lax.axis_index("x"), lax.axis_index("zl")
    sy, sx, sz = source // (X * ZL), source // ZL % X, source % ZL
    held = block
    for to in range(sy + 1, Y):
        sent = lax.ppermute(block, PIPE, [(source, place(to, sx, sz))])
        held = jnp.where(y == to, sent, held)
    column = held
    for to in range(X):
        if to != sx:
            pairs = [(place(k, sx, sz), place(k, to, sz)) for k in range(sy + 1, Y)]
            held = jnp.where(x == to, lax.ppermute(column, PIPE, pairs), held)
    pairs = [
        (place(k, to, sz), place(k, to, 1 - sz)) for k in range(sy + 1, Y) for to in range(X)
    ]
    return jnp.where(zl == sz, held, lax.ppermute(held, PIPE, pairs))


def body(stream, fresh, gain, final_gain, w_query, w_kv, w_out, cache_kv, cache_grad):
    pipe_count, heads = Y * X * ZL, ZH * C
    half = pipe_count // 2
    place_here = lax.axis_index(PIPE)
    section = place_here.astype(jnp.int32)[None]
    depth, width = w_kv.shape[2:]
    tokens = stream.shape[2]
    final_scale = final_gain[None]
    rows8 = (heads, tokens, width)
    columns8 = (heads, width, tokens)
    pair_shape = (tokens, 2 * width)
    flops = 2 * tokens * depth * width * 4
    shift = [(i, i + 1) for i in range(pipe_count - 1)]

    def whole(block):
        return lax.all_gather(block, HEAD, axis=0)

    def exchanged(parts):
        return lax.all_to_all(parts, HEAD, 0, 0, tiled=True)

    def summed(parts, current):
        return (current.astype(F32) + jnp.sum(parts.astype(F32), axis=0)).astype(BF)

    weights = (((depth, width), BF), ((2, depth, width), BF), ((width, depth), BF))
    fresh_whole = whole(fresh)
    current = stream[0].T
    parts, fresh_rows = call(
        functools.partial(first_kernel, half), section,
        (whole(current), fresh, gain, w_query, w_kv, w_out, cache_kv),
        (rows8, (2, tokens, width)),
        ((rows8, BF), ((2, width, tokens), BF), ((2, tokens, width), BF), ((1, depth), F32))
        + weights + ((pair_shape, BF), (rows8, BF), (rows8, BF)),
        8 + heads, flops,
    )

    each = depth // (pipe_count * heads)
    shares = (heads, Y, each, X * ZL, tokens)
    (share,) = call(
        functools.partial(share_kernel, half), section, (cache_grad, w_kv), (shares,),
        ((pair_shape, BF), ((2, depth, width), BF), ((depth, tokens), F32), (shares, F32)),
        3, flops, F32,
    )
    share = share.reshape(depth, tokens)
    share = lax.psum_scatter(share, HEAD, scatter_dimension=0, tiled=True)
    share = lax.psum_scatter(share, "y", scatter_dimension=0, tiled=True)
    share = share.reshape(each, X, ZL, tokens).transpose(1, 2, 0, 3).reshape(X, 1, ZL * each, tokens)
    share = jnp.broadcast_to(share, (X, 8, ZL * each, tokens)).reshape(-1, tokens)
    share = lax.psum_scatter(share, "x", scatter_dimension=0, tiled=True)
    share = share[: ZL * each].reshape(ZL, each, tokens)
    at_first = lax.axis_index("zl") == 0
    kept = jnp.where(at_first, share[0], share[1])
    given = jnp.where(at_first, share[1], share[0])
    memory_grad = kept + lax.ppermute(given, "zl", [(0, 1), (1, 0)])

    output = summed(exchanged(parts), current)
    passed = lax.ppermute(output, PIPE, shift)
    first_memory = spread(output, half - 1)
    entering = output

    current = jnp.where(place_here == 0, fresh_rows[0], passed)
    (parts,) = call(
        functools.partial(second_kernel, half), section,
        (whole(current), fresh_whole, gain, final_scale, w_query, w_kv, w_out, cache_kv),
        (rows8,),
        ((rows8, BF), (columns8, BF), (rows8, BF), ((1, depth), F32), ((1, depth), F32))
        + weights + ((pair_shape, BF), (rows8, BF), (rows8, BF), (rows8, BF)),
        8 + heads, flops,
    )
    current = jnp.where(place_here == half, fresh_rows[1], current)
    output = summed(exchanged(parts), current)
    second_memory = spread(output, half - 1)
    first_memory = whole(jnp.stack([first_memory, entering]))
    passed = lax.ppermute(output, PIPE, shift)
    last = jnp.where(place_here == half, jnp.zeros_like(passed), passed)

    (new_kv,) = call(
        functools.partial(memory_kernel, half), section,
        (first_memory, whole(second_memory), final_scale, w_kv),
        ((1, TICKS, tokens, 2 * width),),
        (((TICKS,) + rows8, BF), ((TICKS,) + rows8, BF), ((1, depth), F32),
         ((2, depth, width), BF), ((TICKS,) + pair_shape, BF)),
        5, flops,
    )
    return (last.T[None], new_kv, memory_grad)


def solution(mesh):
    split = Mesh(mesh.devices.reshape(Y, X, ZL, ZH, C), PIPE + HEAD)
    return jax.shard_map(
        body,
        mesh=split,
        in_specs=(
            P(PIPE, HEAD, None),
            P(None, HEAD, None),
            P(PIPE, None),
            P(),
            P(PIPE, None, HEAD),
            P(PIPE, None, None, HEAD),
            P(PIPE, HEAD, None),
            P(PIPE, None, None, HEAD),
            P(PIPE, None, HEAD),
        ),
        out_specs=(
            P(PIPE, HEAD, None),
            P(PIPE, None, None, HEAD),
            P(PIPE + HEAD, None),
        ),
        check_vma=False,
    )
```

```python
import functools

import jax
import jax.numpy as jnp
from jax import lax
from jax.experimental import pallas as pl
from jax.experimental.pallas import tpu as pltpu
from jax.sharding import Mesh, PartitionSpec as P

TICKS = 2
EPS = 1e-06
PIPE = ("y", "x", "zl")
HEAD = ("zh", "c")
Y, X, ZL, ZH, C = 8, 4, 2, 4, 2
BF, F32 = jnp.bfloat16, jnp.float32


def place(y, x, zl):
    return (y * X + x) * ZL + zl


def norm_into(out, source, scale):
    heads, tokens, width = source.shape
    total = jnp.zeros((tokens, width), F32)
    for h in range(heads):
        wide = source[h].astype(F32)
        total = total + wide * wide
    mean = jnp.sum(total, axis=1, keepdims=True) / (heads * width)
    factor = lax.rsqrt(mean + EPS)
    for h in range(heads):
        wide = source[h].astype(F32)
        out[h] = (wide * factor * scale[:, h * width : (h + 1) * width]).astype(BF)


def project(rows, weight):
    heads, tokens, width = rows.shape
    total = jnp.zeros((tokens, weight.shape[1]), F32)
    for h in range(heads):
        total = total + jnp.dot(
            rows[h], weight[h * width : (h + 1) * width, :], preferred_element_type=F32
        )
    return total.astype(BF)


def attend(query, pair):
    width = query.shape[1]
    scores = lax.dot_general(
        query, pair[:, :width], (((1,), (1,)), ((), ())), preferred_element_type=F32
    )
    scores = scores * width ** (-0.5)
    scores = jnp.exp(scores - jnp.max(scores, axis=-1, keepdims=True))
    probs = (scores / jnp.sum(scores, axis=-1, keepdims=True)).astype(BF)
    return jnp.dot(probs, pair[:, width:], preferred_element_type=F32).astype(BF)


def tick_kernel(tick, half, section, x_hbm, fresh_hbm, gain_hbm, final_hbm, wq_hbm, wkv_hbm, wo_hbm,
                cache_hbm, out_hbm, turned_hbm, x, fresh, turned, gain, final_gain, wq, wkv, wo, pair,
                normed, kv_rows, out, sems):
    heads, tokens, width = x.shape
    here = section[0]
    in_encoder = here < half
    at_half = here == half if tick > 0 else here < 0
    own_pair = jnp.logical_or(in_encoder, at_half)

    def copy(k, source, target):
        return pltpu.make_async_copy(source, target, sems.at[k])

    get_x = copy(0, x_hbm, x)
    get_gain = copy(1, gain_hbm, gain)
    get_wq = copy(2, wq_hbm.at[0], wq)
    get_wkv = copy(3, wkv_hbm.at[0], wkv)
    get_cache = copy(4, cache_hbm.at[0, tick], pair)
    get_wo = copy(5, wo_hbm.at[0], wo)
    get_x.start()
    get_gain.start()
    get_wq.start()
    pl.when(own_pair)(get_wkv.start)
    pl.when(jnp.logical_not(own_pair))(get_cache.start)
    get_wo.start()
    if tick == 0:
        get_fresh = copy(6, fresh_hbm, fresh)
        get_fresh.start()
    get_x.wait()
    get_gain.wait()
    if tick == 0:
        norm_into(normed, x, gain)
        get_fresh.wait()
        for h in range(fresh.shape[0]):
            turned[h] = fresh[h].T
        put_turned = copy(7, turned, turned_hbm)
        put_turned.start()
    else:
        get_fresh = copy(6, fresh_hbm.at[:, 1], fresh)
        get_final = copy(7, final_hbm, final_gain)

        @pl.when(at_half)
        def _():
            get_fresh.start()
            get_final.start()
            get_fresh.wait()
            get_final.wait()
            for h in range(heads):
                turned[h] = fresh[h].T
            norm_into(normed, turned, gain)
            norm_into(kv_rows, x, final_gain)

        @pl.when(jnp.logical_not(at_half))
        def _():
            norm_into(normed, x, gain)

    get_wq.wait()
    query = project(normed, wq)

    @pl.when(in_encoder)
    def _():
        get_wkv.wait()
        pair[:, :width] = project(normed, wkv.at[0])
        pair[:, width:] = project(normed, wkv.at[1])

    if tick > 0:

        @pl.when(at_half)
        def _():
            get_wkv.wait()
            pair[:, :width] = project(kv_rows, wkv.at[0])
            pair[:, width:] = project(kv_rows, wkv.at[1])

    @pl.when(jnp.logical_not(own_pair))
    def _():
        get_cache.wait()

    attn = attend(query, pair)
    get_wo.wait()
    puts = []
    for h in range(heads):
        out[h] = jnp.dot(
            attn, wo[:, h * width : (h + 1) * width], preferred_element_type=F32
        ).astype(BF)
        puts.append(copy(8 + h, out.at[h], out_hbm.at[h]))
        puts[-1].start()
    if tick == 0:
        put_turned.wait()
    for put in puts:
        put.wait()


def first_kernel(half, section, x, fresh, gain, wq, wkv, wo, cache, out, turned, *scratch):
    scratch = scratch[:4] + (None,) + scratch[4:9] + (None,) + scratch[9:]
    tick_kernel(0, half, section, x, fresh, gain, None, wq, wkv, wo, cache, out, turned, *scratch)


def second_kernel(half, section, x, fresh, gain, final, wq, wkv, wo, cache, out, *scratch):
    tick_kernel(1, half, section, x, fresh, gain, final, wq, wkv, wo, cache, out, None, *scratch)


def share_kernel(half, section, grads_hbm, wkv_hbm, out_hbm, grads, wkv, out, sems):
    width = wkv.shape[2]

    @pl.when(section[0] >= half)
    def _():
        get_grads = pltpu.make_async_copy(grads_hbm.at[0], grads, sems.at[0])
        get_wkv = pltpu.make_async_copy(wkv_hbm.at[0], wkv, sems.at[1])
        get_grads.start()
        get_wkv.start()
        get_grads.wait()
        get_wkv.wait()
        rows_by = (((1,), (1,)), ((), ()))
        out[...] = lax.dot_general(
            wkv[0], grads[:, :width], rows_by, preferred_element_type=F32
        ) + lax.dot_general(wkv[1], grads[:, width:], rows_by, preferred_element_type=F32)

    @pl.when(section[0] < half)
    def _():
        out[...] = jnp.zeros_like(out)

    put = pltpu.make_async_copy(out, out_hbm, sems.at[2])
    put.start()
    put.wait()


def memory_kernel(half, section, first_hbm, second_hbm, final_hbm, wkv_hbm, out_hbm, sources, rows,
                  final_gain, wkv, out, sems):
    width = wkv.shape[2]

    def copy(k, source, target):
        return pltpu.make_async_copy(source, target, sems.at[k])

    gets = [
        copy(0, second_hbm, sources.at[1]),
        copy(1, final_hbm, final_gain),
        copy(2, first_hbm.at[:, 0], sources.at[0]),
        copy(3, wkv_hbm.at[0], wkv),
    ]

    @pl.when(section[0] >= half)
    def _():
        for get in gets:
            get.start()
        for get in gets[:3]:
            get.wait()
        for t in range(TICKS):
            norm_into(rows.at[t], sources.at[t], final_gain)
        gets[3].wait()
        for t in range(TICKS):
            out[t, :, :width] = project(rows.at[t], wkv.at[0])
            out[t, :, width:] = project(rows.at[t], wkv.at[1])

    @pl.when(section[0] < half)
    def _():
        out[...] = jnp.zeros_like(out)

    put = copy(4, out, out_hbm.at[0])
    put.start()
    put.wait()


def call(kernel, section, operands, out_shapes, scratch, copies, flops, kind=BF):
    return pl.pallas_call(
        kernel,
        out_shape=[jax.ShapeDtypeStruct(shape, kind) for shape in out_shapes],
        in_specs=[pl.BlockSpec(memory_space=pltpu.SMEM)]
        + [pl.BlockSpec(memory_space=pl.ANY)] * len(operands),
        out_specs=[pl.BlockSpec(memory_space=pl.ANY)] * len(out_shapes),
        scratch_shapes=[pltpu.VMEM(shape, held) for shape, held in scratch]
        + [pltpu.SemaphoreType.DMA((copies,))],
        compiler_params=pltpu.CompilerParams(vmem_limit_bytes=60 * 1024 * 1024),
        cost_estimate=pl.CostEstimate(flops=flops, bytes_accessed=5_000_000, transcendentals=0),
    )(section, *operands)


def spread(block, source, beside):
    y, x, zl = lax.axis_index("y"), lax.axis_index("x"), lax.axis_index("zl")
    sy, sx, sz = source // (X * ZL), source // ZL % X, source % ZL
    held = block
    for to in range(sy + 1, Y):
        sent = lax.ppermute(block, PIPE, [(source, place(to, sx, sz))])
        held = jnp.where(y == to, sent, held)
    column = held
    for to in range(X):
        if to != sx:
            pairs = [(place(k, sx, sz), place(k, to, sz)) for k in range(sy + 1, Y)]
            held = jnp.where(x == to, lax.ppermute(column, PIPE, pairs), held)
    if beside is not None:
        held, beside = lax.optimization_barrier((held, beside))
    pairs = [
        (place(k, to, sz), place(k, to, 1 - sz)) for k in range(sy + 1, Y) for to in range(X)
    ]
    return jnp.where(zl == sz, held, lax.ppermute(held, PIPE, pairs)), beside


def body(stream, fresh, gain, final_gain, w_query, w_kv, w_out, cache_kv, cache_grad):
    pipe_count, heads = Y * X * ZL, ZH * C
    half = pipe_count // 2
    place_here = lax.axis_index(PIPE)
    section = place_here.astype(jnp.int32)[None]
    depth, width = w_kv.shape[2:]
    tokens = stream.shape[2]
    final_scale = final_gain[None]
    rows8 = (heads, tokens, width)
    columns8 = (heads, width, tokens)
    pair_shape = (tokens, 2 * width)
    flops = 2 * tokens * depth * width * 4
    shift = [(i, i + 1) for i in range(pipe_count - 1)]

    def whole(block):
        return lax.all_gather(block, HEAD, axis=0)

    def exchanged(parts):
        return lax.all_to_all(parts, HEAD, 0, 0, tiled=True)

    def summed(parts, current):
        return (current.astype(F32) + jnp.sum(parts.astype(F32), axis=0)).astype(BF)

    weights = (((depth, width), BF), ((2, depth, width), BF), ((width, depth), BF))
    fresh_whole = whole(fresh)
    current = stream[0].T
    parts, fresh_rows = call(
        functools.partial(first_kernel, half), section,
        (whole(current), fresh, gain, w_query, w_kv, w_out, cache_kv),
        (rows8, (2, tokens, width)),
        ((rows8, BF), ((2, width, tokens), BF), ((2, tokens, width), BF), ((1, depth), F32))
        + weights + ((pair_shape, BF), (rows8, BF), (rows8, BF)),
        8 + heads, flops,
    )

    (share,) = call(
        functools.partial(share_kernel, half), section, (cache_grad, w_kv), ((depth, tokens),),
        ((pair_shape, BF), ((2, depth, width), BF), ((depth, tokens), F32)),
        3, flops, F32,
    )
    share = lax.psum_scatter(share, "y", scatter_dimension=0, tiled=True)
    plane = X * ZL * heads
    share = share.reshape(plane, depth // (pipe_count * heads), tokens)

    output = summed(exchanged(parts), current)
    passed = lax.ppermute(output, PIPE, shift)
    first_memory, _ = spread(output, half - 1, None)
    entering = output

    current = jnp.where(place_here == 0, fresh_rows[0], passed)
    (parts,) = call(
        functools.partial(second_kernel, half), section,
        (whole(current), fresh_whole, gain, final_scale, w_query, w_kv, w_out, cache_kv),
        (rows8,),
        ((rows8, BF), (columns8, BF), (rows8, BF), ((1, depth), F32), ((1, depth), F32))
        + weights + ((pair_shape, BF), (rows8, BF), (rows8, BF), (rows8, BF)),
        8 + heads, flops,
    )
    current = jnp.where(place_here == half, fresh_rows[1], current)
    parts, first_memory = lax.optimization_barrier((exchanged(parts), first_memory))
    output = summed(parts, current)
    second_memory, share = spread(output, half - 1, share)
    share = lax.all_to_all(share, PIPE[1:] + HEAD, 0, 0, tiled=True)
    first_memory = whole(jnp.stack([first_memory, entering]))
    passed = lax.ppermute(output, PIPE, shift)
    last = jnp.where(place_here == half, jnp.zeros_like(passed), passed)
    share, second_memory = lax.optimization_barrier((share, whole(second_memory)))
    memory_grad = jnp.sum(share, axis=0)

    (new_kv,) = call(
        functools.partial(memory_kernel, half), section,
        (first_memory, second_memory, final_scale, w_kv),
        ((1, TICKS, tokens, 2 * width),),
        (((TICKS,) + rows8, BF), ((TICKS,) + rows8, BF), ((1, depth), F32),
         ((2, depth, width), BF), ((TICKS,) + pair_shape, BF)),
        5, flops,
    )
    return (last.T[None], new_kv, memory_grad)


def solution(mesh):
    split = Mesh(mesh.devices.reshape(Y, X, ZL, ZH, C), PIPE + HEAD)
    return jax.shard_map(
        body,
        mesh=split,
        in_specs=(
            P(PIPE, HEAD, None),
            P(None, HEAD, None),
            P(PIPE, None),
            P(),
            P(PIPE, None, HEAD),
            P(PIPE, None, None, HEAD),
            P(PIPE, HEAD, None),
            P(PIPE, None, None, HEAD),
            P(PIPE, None, HEAD),
        ),
        out_specs=(
            P(PIPE, HEAD, None),
            P(PIPE, None, None, HEAD),
            P(PIPE + HEAD, None),
        ),
        check_vma=False,
    )
```

```python
import functools

import jax
import jax.numpy as jnp
from jax import lax
from jax.experimental import pallas as pl
from jax.experimental.pallas import tpu as pltpu
from jax.sharding import Mesh, PartitionSpec as P

TICKS = 2
EPS = 1e-06
PIPE = ("y", "x", "zl")
HEAD = ("zh", "c")
Y, X, ZL, ZH, C = 8, 4, 2, 4, 2
BF, F32 = jnp.bfloat16, jnp.float32


def place(y, x, zl):
    return (y * X + x) * ZL + zl


def norm_into(out, source, scale):
    heads, tokens, width = source.shape
    total = jnp.zeros((tokens, width), F32)
    for h in range(heads):
        wide = source[h].astype(F32)
        total = total + wide * wide
    mean = jnp.sum(total, axis=1, keepdims=True) / (heads * width)
    factor = lax.rsqrt(mean + EPS)
    for h in range(heads):
        wide = source[h].astype(F32)
        out[h] = (wide * factor * scale[:, h * width : (h + 1) * width]).astype(BF)


def project(rows, weight):
    heads, tokens, width = rows.shape
    total = jnp.zeros((tokens, weight.shape[1]), F32)
    for h in range(heads):
        total = total + jnp.dot(
            rows[h], weight[h * width : (h + 1) * width, :], preferred_element_type=F32
        )
    return total.astype(BF)


def attend(query, pair):
    width = query.shape[1]
    scores = lax.dot_general(
        query, pair[:, :width], (((1,), (1,)), ((), ())), preferred_element_type=F32
    )
    scores = scores * width ** (-0.5)
    scores = jnp.exp(scores - jnp.max(scores, axis=-1, keepdims=True))
    probs = (scores / jnp.sum(scores, axis=-1, keepdims=True)).astype(BF)
    return jnp.dot(probs, pair[:, width:], preferred_element_type=F32).astype(BF)


def tick_kernel(tick, half, section, x_hbm, fresh_hbm, gain_hbm, final_hbm, wq_hbm, wkv_hbm, wo_hbm,
                cache_hbm, out_hbm, turned_hbm, x, fresh, turned, gain, final_gain, wq, wkv, wo, pair,
                normed, kv_rows, out, sems):
    heads, tokens, width = x.shape
    here = section[0]
    in_encoder = here < half
    at_half = here == half if tick > 0 else here < 0
    own_pair = jnp.logical_or(in_encoder, at_half)

    def copy(k, source, target):
        return pltpu.make_async_copy(source, target, sems.at[k])

    get_x = copy(0, x_hbm, x)
    get_gain = copy(1, gain_hbm, gain)
    get_wq = copy(2, wq_hbm.at[0], wq)
    get_wkv = copy(3, wkv_hbm.at[0], wkv)
    get_cache = copy(4, cache_hbm.at[0, tick], pair)
    get_wo = copy(5, wo_hbm.at[0], wo)
    get_x.start()
    get_gain.start()
    get_wq.start()
    pl.when(own_pair)(get_wkv.start)
    pl.when(jnp.logical_not(own_pair))(get_cache.start)
    get_wo.start()
    if tick == 0:
        get_fresh = copy(6, fresh_hbm, fresh)
        get_fresh.start()
    get_x.wait()
    get_gain.wait()
    if tick == 0:
        norm_into(normed, x, gain)
        get_fresh.wait()
        for h in range(fresh.shape[0]):
            turned[h] = fresh[h].T
        put_turned = copy(7, turned, turned_hbm)
        put_turned.start()
    else:
        get_fresh = copy(6, fresh_hbm.at[:, 1], fresh)
        get_final = copy(7, final_hbm, final_gain)

        @pl.when(at_half)
        def _():
            get_fresh.start()
            get_final.start()
            get_fresh.wait()
            get_final.wait()
            for h in range(heads):
                turned[h] = fresh[h].T
            norm_into(normed, turned, gain)
            norm_into(kv_rows, x, final_gain)

        @pl.when(jnp.logical_not(at_half))
        def _():
            norm_into(normed, x, gain)

    get_wq.wait()
    query = project(normed, wq)

    @pl.when(in_encoder)
    def _():
        get_wkv.wait()
        pair[:, :width] = project(normed, wkv.at[0])
        pair[:, width:] = project(normed, wkv.at[1])

    if tick > 0:

        @pl.when(at_half)
        def _():
            get_wkv.wait()
            pair[:, :width] = project(kv_rows, wkv.at[0])
            pair[:, width:] = project(kv_rows, wkv.at[1])

    @pl.when(jnp.logical_not(own_pair))
    def _():
        get_cache.wait()

    attn = attend(query, pair)
    get_wo.wait()
    puts = []
    for h in range(heads):
        out[h] = jnp.dot(
            attn, wo[:, h * width : (h + 1) * width], preferred_element_type=F32
        ).astype(BF)
        puts.append(copy(8 + h, out.at[h], out_hbm.at[h]))
        puts[-1].start()
    if tick == 0:
        put_turned.wait()
    for put in puts:
        put.wait()


def first_kernel(half, section, x, fresh, gain, wq, wkv, wo, cache, out, turned, *scratch):
    scratch = scratch[:4] + (None,) + scratch[4:9] + (None,) + scratch[9:]
    tick_kernel(0, half, section, x, fresh, gain, None, wq, wkv, wo, cache, out, turned, *scratch)


def second_kernel(half, section, x, fresh, gain, final, wq, wkv, wo, cache, out, *scratch):
    tick_kernel(1, half, section, x, fresh, gain, final, wq, wkv, wo, cache, out, None, *scratch)


def share_kernel(half, section, grads_hbm, wkv_hbm, out_hbm, grads, wkv, out, sems):
    width = wkv.shape[2]

    @pl.when(section[0] >= half)
    def _():
        get_grads = pltpu.make_async_copy(grads_hbm.at[0], grads, sems.at[0])
        get_wkv = pltpu.make_async_copy(wkv_hbm.at[0], wkv, sems.at[1])
        get_grads.start()
        get_wkv.start()
        get_grads.wait()
        get_wkv.wait()
        rows_by = (((1,), (1,)), ((), ()))
        out[...] = lax.dot_general(
            wkv[0], grads[:, :width], rows_by, preferred_element_type=F32
        ) + lax.dot_general(wkv[1], grads[:, width:], rows_by, preferred_element_type=F32)

    @pl.when(section[0] < half)
    def _():
        out[...] = jnp.zeros_like(out)

    put = pltpu.make_async_copy(out, out_hbm, sems.at[2])
    put.start()
    put.wait()


def memory_kernel(half, section, first_hbm, second_hbm, final_hbm, wkv_hbm, out_hbm, sources, rows,
                  final_gain, wkv, out, sems):
    width = wkv.shape[2]

    def copy(k, source, target):
        return pltpu.make_async_copy(source, target, sems.at[k])

    gets = [
        copy(0, second_hbm, sources.at[1]),
        copy(1, final_hbm, final_gain),
        copy(2, first_hbm.at[:, 0], sources.at[0]),
        copy(3, wkv_hbm.at[0], wkv),
    ]

    @pl.when(section[0] >= half)
    def _():
        for get in gets:
            get.start()
        for get in gets[:3]:
            get.wait()
        for t in range(TICKS):
            norm_into(rows.at[t], sources.at[t], final_gain)
        gets[3].wait()
        for t in range(TICKS):
            out[t, :, :width] = project(rows.at[t], wkv.at[0])
            out[t, :, width:] = project(rows.at[t], wkv.at[1])

    @pl.when(section[0] < half)
    def _():
        out[...] = jnp.zeros_like(out)

    put = copy(4, out, out_hbm.at[0])
    put.start()
    put.wait()


def call(kernel, section, operands, out_shapes, scratch, copies, flops, kind=BF):
    return pl.pallas_call(
        kernel,
        out_shape=[jax.ShapeDtypeStruct(shape, kind) for shape in out_shapes],
        in_specs=[pl.BlockSpec(memory_space=pltpu.SMEM)]
        + [pl.BlockSpec(memory_space=pl.ANY)] * len(operands),
        out_specs=[pl.BlockSpec(memory_space=pl.ANY)] * len(out_shapes),
        scratch_shapes=[pltpu.VMEM(shape, held) for shape, held in scratch]
        + [pltpu.SemaphoreType.DMA((copies,))],
        compiler_params=pltpu.CompilerParams(vmem_limit_bytes=60 * 1024 * 1024),
        cost_estimate=pl.CostEstimate(flops=flops, bytes_accessed=5_000_000, transcendentals=0),
    )(section, *operands)


def spread(block, source, rows, beside):
    y, x, zl = lax.axis_index("y"), lax.axis_index("x"), lax.axis_index("zl")
    sy, sx, sz = source // (X * ZL), source // ZL % X, source % ZL
    held = block
    for to in rows:
        if to != sy:
            sent = lax.ppermute(block, PIPE, [(source, place(to, sx, sz))])
            held = jnp.where(y == to, sent, held)
    column, beside = lax.optimization_barrier((held, beside))
    held = column
    for to in range(X):
        if to != sx:
            pairs = [(place(k, sx, sz), place(k, to, sz)) for k in rows]
            held = jnp.where(x == to, lax.ppermute(column, PIPE, pairs), held)
    pairs = [(place(k, to, sz), place(k, to, 1 - sz)) for k in rows for to in range(X)]
    return jnp.where(zl == sz, held, lax.ppermute(held, PIPE, pairs)), beside


def body(stream, fresh, gain, final_gain, w_query, w_kv, w_out, cache_kv, cache_grad):
    pipe_count, heads = Y * X * ZL, ZH * C
    half = pipe_count // 2
    place_here = lax.axis_index(PIPE)
    section = place_here.astype(jnp.int32)[None]
    depth, width = w_kv.shape[2:]
    tokens = stream.shape[2]
    final_scale = final_gain[None]
    rows8 = (heads, tokens, width)
    columns8 = (heads, width, tokens)
    pair_shape = (tokens, 2 * width)
    flops = 2 * tokens * depth * width * 4
    shift = [(i, i + 1) for i in range(pipe_count - 1)]

    def whole(block):
        return lax.all_gather(block, HEAD, axis=0)

    def exchanged(parts):
        return lax.all_to_all(parts, HEAD, 0, 0, tiled=True)

    def summed(parts, current):
        return (current.astype(F32) + jnp.sum(parts.astype(F32), axis=0)).astype(BF)

    weights = (((depth, width), BF), ((2, depth, width), BF), ((width, depth), BF))
    fresh_whole = whole(fresh)
    current = stream[0].T
    parts, fresh_rows = call(
        functools.partial(first_kernel, half), section,
        (whole(current), fresh, gain, w_query, w_kv, w_out, cache_kv),
        (rows8, (2, tokens, width)),
        ((rows8, BF), ((2, width, tokens), BF), ((2, tokens, width), BF), ((1, depth), F32))
        + weights + ((pair_shape, BF), (rows8, BF), (rows8, BF)),
        8 + heads, flops,
    )

    (share,) = call(
        functools.partial(share_kernel, half), section, (cache_grad, w_kv), ((depth, tokens),),
        ((pair_shape, BF), ((2, depth, width), BF), ((depth, tokens), F32)),
        3, flops, F32,
    )
    share = lax.psum_scatter(share, "y", scatter_dimension=0, tiled=True)
    plane = X * ZL * heads
    share = share.reshape(plane, depth // (pipe_count * heads), tokens)

    output = summed(exchanged(parts), current)
    passed = lax.ppermute(output, PIPE, shift)
    entering = output

    rows = range(half // (X * ZL), Y)
    current = jnp.where(place_here == 0, fresh_rows[0], passed)
    first_memory, current = spread(passed, half, rows, current)
    (parts,) = call(
        functools.partial(second_kernel, half), section,
        (whole(current), fresh_whole, gain, final_scale, w_query, w_kv, w_out, cache_kv),
        (rows8,),
        ((rows8, BF), (columns8, BF), (rows8, BF), ((1, depth), F32), ((1, depth), F32))
        + weights + ((pair_shape, BF), (rows8, BF), (rows8, BF), (rows8, BF)),
        8 + heads, flops,
    )
    current = jnp.where(place_here == half, fresh_rows[1], current)
    parts, first_memory = lax.optimization_barrier((exchanged(parts), first_memory))
    output = summed(parts, current)
    second_memory, share = spread(output, half - 1, rows, share)
    share = lax.all_to_all(share, PIPE[1:] + HEAD, 0, 0, tiled=True)
    first_memory = whole(jnp.stack([first_memory, entering]))
    passed = lax.ppermute(output, PIPE, shift)
    last = jnp.where(place_here == half, jnp.zeros_like(passed), passed)
    share, second_memory = lax.optimization_barrier((share, whole(second_memory)))
    memory_grad = jnp.sum(share, axis=0)

    (new_kv,) = call(
        functools.partial(memory_kernel, half), section,
        (first_memory, second_memory, final_scale, w_kv),
        ((1, TICKS, tokens, 2 * width),),
        (((TICKS,) + rows8, BF), ((TICKS,) + rows8, BF), ((1, depth), F32),
         ((2, depth, width), BF), ((TICKS,) + pair_shape, BF)),
        5, flops,
    )
    return (last.T[None], new_kv, memory_grad)


def solution(mesh):
    split = Mesh(mesh.devices.reshape(Y, X, ZL, ZH, C), PIPE + HEAD)
    return jax.shard_map(
        body,
        mesh=split,
        in_specs=(
            P(PIPE, HEAD, None),
            P(None, HEAD, None),
            P(PIPE, None),
            P(),
            P(PIPE, None, HEAD),
            P(PIPE, None, None, HEAD),
            P(PIPE, HEAD, None),
            P(PIPE, None, None, HEAD),
            P(PIPE, None, HEAD),
        ),
        out_specs=(
            P(PIPE, HEAD, None),
            P(PIPE, None, None, HEAD),
            P(PIPE + HEAD, None),
        ),
        check_vma=False,
    )
```

```python
import functools

import jax
import jax.numpy as jnp
from jax import lax
from jax.experimental import pallas as pl
from jax.experimental.pallas import tpu as pltpu
from jax.sharding import Mesh, PartitionSpec as P

TICKS = 2
EPS = 1e-06
PIPE = ("y", "x", "zl")
HEAD = ("zh", "c")
Y, X, ZL, ZH, C = 8, 4, 2, 4, 2
BF, F32 = jnp.bfloat16, jnp.float32


def place(y, x, zl):
    return (y * X + x) * ZL + zl


def norm_into(out, source, scale):
    heads, tokens, width = source.shape
    total = jnp.zeros((tokens, width), F32)
    for h in range(heads):
        wide = source[h].astype(F32)
        total = total + wide * wide
    mean = jnp.sum(total, axis=1, keepdims=True) / (heads * width)
    factor = lax.rsqrt(mean + EPS)
    for h in range(heads):
        wide = source[h].astype(F32)
        out[h] = (wide * factor * scale[:, h * width : (h + 1) * width]).astype(BF)


def project(rows, weight):
    heads, tokens, width = rows.shape
    total = jnp.zeros((tokens, weight.shape[1]), F32)
    for h in range(heads):
        total = total + jnp.dot(
            rows[h], weight[h * width : (h + 1) * width, :], preferred_element_type=F32
        )
    return total.astype(BF)


def attend(query, pair):
    width = query.shape[1]
    scores = lax.dot_general(
        query, pair[:, :width], (((1,), (1,)), ((), ())), preferred_element_type=F32
    )
    scores = scores * width ** (-0.5)
    scores = jnp.exp(scores - jnp.max(scores, axis=-1, keepdims=True))
    probs = (scores / jnp.sum(scores, axis=-1, keepdims=True)).astype(BF)
    return jnp.dot(probs, pair[:, width:], preferred_element_type=F32).astype(BF)


def tick_kernel(tick, half, section, x_hbm, fresh_hbm, gain_hbm, final_hbm, wq_hbm, wkv_hbm, wo_hbm,
                cache_hbm, out_hbm, turned_hbm, x, fresh, turned, gain, final_gain, wq, wkv, wo, pair,
                normed, kv_rows, out, sems):
    heads, tokens, width = x.shape
    here = section[0]
    in_encoder = here < half
    at_half = here == half if tick > 0 else here < 0
    own_pair = jnp.logical_or(in_encoder, at_half)

    def copy(k, source, target):
        return pltpu.make_async_copy(source, target, sems.at[k])

    get_x = copy(0, x_hbm, x)
    get_gain = copy(1, gain_hbm, gain)
    get_wq = copy(2, wq_hbm.at[0], wq)
    get_wkv = copy(3, wkv_hbm.at[0], wkv)
    get_cache = copy(4, cache_hbm.at[0, tick], pair)
    get_wo = copy(5, wo_hbm.at[0], wo)
    get_x.start()
    get_gain.start()
    get_wq.start()
    pl.when(own_pair)(get_wkv.start)
    pl.when(jnp.logical_not(own_pair))(get_cache.start)
    get_wo.start()
    if tick == 0:
        get_fresh = copy(6, fresh_hbm, fresh)
        get_fresh.start()
    get_x.wait()
    get_gain.wait()
    if tick == 0:
        norm_into(normed, x, gain)
        get_fresh.wait()
        for h in range(fresh.shape[0]):
            turned[h] = fresh[h].T
        put_turned = copy(7, turned, turned_hbm)
        put_turned.start()
    else:
        get_fresh = copy(6, fresh_hbm.at[:, 1], fresh)
        get_final = copy(7, final_hbm, final_gain)

        @pl.when(at_half)
        def _():
            get_fresh.start()
            get_final.start()
            get_fresh.wait()
            get_final.wait()
            for h in range(heads):
                turned[h] = fresh[h].T
            norm_into(normed, turned, gain)
            norm_into(kv_rows, x, final_gain)

        @pl.when(jnp.logical_not(at_half))
        def _():
            norm_into(normed, x, gain)

    get_wq.wait()
    query = project(normed, wq)

    @pl.when(in_encoder)
    def _():
        get_wkv.wait()
        pair[:, :width] = project(normed, wkv.at[0])
        pair[:, width:] = project(normed, wkv.at[1])

    if tick > 0:

        @pl.when(at_half)
        def _():
            get_wkv.wait()
            pair[:, :width] = project(kv_rows, wkv.at[0])
            pair[:, width:] = project(kv_rows, wkv.at[1])

    @pl.when(jnp.logical_not(own_pair))
    def _():
        get_cache.wait()

    attn = attend(query, pair)
    get_wo.wait()
    puts = []
    for h in range(heads):
        out[h] = jnp.dot(
            attn, wo[:, h * width : (h + 1) * width], preferred_element_type=F32
        ).astype(BF)
        puts.append(copy(8 + h, out.at[h], out_hbm.at[h]))
        puts[-1].start()
    if tick == 0:
        put_turned.wait()
    for put in puts:
        put.wait()


def first_kernel(half, section, x, fresh, gain, wq, wkv, wo, cache, out, turned, *scratch):
    scratch = scratch[:4] + (None,) + scratch[4:9] + (None,) + scratch[9:]
    tick_kernel(0, half, section, x, fresh, gain, None, wq, wkv, wo, cache, out, turned, *scratch)


def second_kernel(half, section, x, fresh, gain, final, wq, wkv, wo, cache, out, *scratch):
    tick_kernel(1, half, section, x, fresh, gain, final, wq, wkv, wo, cache, out, None, *scratch)


def share_kernel(half, section, grads_hbm, wkv_hbm, out_hbm, grads, wkv, out, sems):
    width = wkv.shape[2]

    @pl.when(section[0] >= half)
    def _():
        get_grads = pltpu.make_async_copy(grads_hbm.at[0], grads, sems.at[0])
        get_wkv = pltpu.make_async_copy(wkv_hbm.at[0], wkv, sems.at[1])
        get_grads.start()
        get_wkv.start()
        get_grads.wait()
        get_wkv.wait()
        rows_by = (((1,), (1,)), ((), ()))
        out[...] = lax.dot_general(
            wkv[0], grads[:, :width], rows_by, preferred_element_type=F32
        ) + lax.dot_general(wkv[1], grads[:, width:], rows_by, preferred_element_type=F32)

    @pl.when(section[0] < half)
    def _():
        out[...] = jnp.zeros_like(out)

    put = pltpu.make_async_copy(out, out_hbm, sems.at[2])
    put.start()
    put.wait()


def memory_kernel(half, section, first_hbm, second_hbm, final_hbm, wkv_hbm, out_hbm, sources, rows,
                  final_gain, wkv, out, sems):
    width = wkv.shape[2]
    heads = sources.shape[1]

    def copy(k, source, target):
        return pltpu.make_async_copy(source, target, sems.at[k])

    gets = [
        copy(0, second_hbm, sources.at[1]),
        copy(1, final_hbm, final_gain),
        copy(2, first_hbm.at[pl.ds((half - 1) % ZL * heads, heads)], sources.at[0]),
        copy(3, wkv_hbm.at[0], wkv),
    ]

    @pl.when(section[0] >= half)
    def _():
        for get in gets:
            get.start()
        for get in gets[:3]:
            get.wait()
        for t in range(TICKS):
            norm_into(rows.at[t], sources.at[t], final_gain)
        gets[3].wait()
        for t in range(TICKS):
            out[t, :, :width] = project(rows.at[t], wkv.at[0])
            out[t, :, width:] = project(rows.at[t], wkv.at[1])

    @pl.when(section[0] < half)
    def _():
        out[...] = jnp.zeros_like(out)

    put = copy(4, out, out_hbm.at[0])
    put.start()
    put.wait()


def call(kernel, section, operands, out_shapes, scratch, copies, flops, kind=BF):
    return pl.pallas_call(
        kernel,
        out_shape=[jax.ShapeDtypeStruct(shape, kind) for shape in out_shapes],
        in_specs=[pl.BlockSpec(memory_space=pltpu.SMEM)]
        + [pl.BlockSpec(memory_space=pl.ANY)] * len(operands),
        out_specs=[pl.BlockSpec(memory_space=pl.ANY)] * len(out_shapes),
        scratch_shapes=[pltpu.VMEM(shape, held) for shape, held in scratch]
        + [pltpu.SemaphoreType.DMA((copies,))],
        compiler_params=pltpu.CompilerParams(vmem_limit_bytes=60 * 1024 * 1024),
        cost_estimate=pl.CostEstimate(flops=flops, bytes_accessed=5_000_000, transcendentals=0),
    )(section, *operands)


def spread(block, source):
    y, x = lax.axis_index("y"), lax.axis_index("x")
    sy, sx, sz = source // (X * ZL), source // ZL % X, source % ZL
    held = block
    for to in range(sy + 1, Y):
        sent = lax.ppermute(block, PIPE, [(source, place(to, sx, sz))])
        held = jnp.where(y == to, sent, held)
    column = held
    for to in range(X):
        if to != sx:
            pairs = [(place(k, sx, sz), place(k, to, sz)) for k in range(sy + 1, Y)]
            held = jnp.where(x == to, lax.ppermute(column, PIPE, pairs), held)
    return held


def spread_zl(held, source):
    sy, sz = source // (X * ZL), source % ZL
    pairs = [
        (place(k, to, sz), place(k, to, 1 - sz)) for k in range(sy + 1, Y) for to in range(X)
    ]
    return jnp.where(lax.axis_index("zl") == sz, held, lax.ppermute(held, PIPE, pairs))


def body(stream, fresh, gain, final_gain, w_query, w_kv, w_out, cache_kv, cache_grad):
    pipe_count, heads = Y * X * ZL, ZH * C
    half = pipe_count // 2
    place_here = lax.axis_index(PIPE)
    section = place_here.astype(jnp.int32)[None]
    depth, width = w_kv.shape[2:]
    tokens = stream.shape[2]
    final_scale = final_gain[None]
    rows8 = (heads, tokens, width)
    columns8 = (heads, width, tokens)
    pair_shape = (tokens, 2 * width)
    flops = 2 * tokens * depth * width * 4
    shift = [(i, i + 1) for i in range(pipe_count - 1)]

    def whole(block):
        return lax.all_gather(block, HEAD, axis=0)

    def exchanged(parts):
        return lax.all_to_all(parts, HEAD, 0, 0, tiled=True)

    def summed(parts, current):
        return (current.astype(F32) + jnp.sum(parts.astype(F32), axis=0)).astype(BF)

    weights = (((depth, width), BF), ((2, depth, width), BF), ((width, depth), BF))
    fresh_whole = whole(fresh)
    current = stream[0].T
    parts, fresh_rows = call(
        functools.partial(first_kernel, half), section,
        (whole(current), fresh, gain, w_query, w_kv, w_out, cache_kv),
        (rows8, (2, tokens, width)),
        ((rows8, BF), ((2, width, tokens), BF), ((2, tokens, width), BF), ((1, depth), F32))
        + weights + ((pair_shape, BF), (rows8, BF), (rows8, BF)),
        8 + heads, flops,
    )

    (share,) = call(
        functools.partial(share_kernel, half), section, (cache_grad, w_kv), ((depth, tokens),),
        ((pair_shape, BF), ((2, depth, width), BF), ((depth, tokens), F32)),
        3, flops, F32,
    )
    share = lax.psum_scatter(share, "y", scatter_dimension=0, tiled=True)
    plane = X * ZL * heads
    share = share.reshape(plane, depth // (pipe_count * heads), tokens)

    output = summed(exchanged(parts), current)
    passed = lax.ppermute(output, PIPE, shift)
    first_memory = spread(output, half - 1)

    current = jnp.where(place_here == 0, fresh_rows[0], passed)
    (parts,) = call(
        functools.partial(second_kernel, half), section,
        (whole(current), fresh_whole, gain, final_scale, w_query, w_kv, w_out, cache_kv),
        (rows8,),
        ((rows8, BF), (columns8, BF), (rows8, BF), ((1, depth), F32), ((1, depth), F32))
        + weights + ((pair_shape, BF), (rows8, BF), (rows8, BF), (rows8, BF)),
        8 + heads, flops,
    )
    current = jnp.where(place_here == half, fresh_rows[1], current)
    parts, first_memory = lax.optimization_barrier((exchanged(parts), first_memory))
    output = summed(parts, current)
    first_memory = lax.all_gather(first_memory, ("zl",) + HEAD, axis=0)
    second_memory = whole(spread_zl(spread(output, half - 1), half - 1))
    passed = lax.ppermute(output, PIPE, shift)
    last = jnp.where(place_here == half, jnp.zeros_like(passed), passed)
    share, second_memory = lax.optimization_barrier((share, second_memory))
    share = lax.all_to_all(share, PIPE[1:] + HEAD, 0, 0, tiled=True)
    memory_grad = jnp.sum(share, axis=0)

    (new_kv,) = call(
        functools.partial(memory_kernel, half), section,
        (first_memory, second_memory, final_scale, w_kv),
        ((1, TICKS, tokens, 2 * width),),
        (((TICKS,) + rows8, BF), ((TICKS,) + rows8, BF), ((1, depth), F32),
         ((2, depth, width), BF), ((TICKS,) + pair_shape, BF)),
        5, flops,
    )
    return (last.T[None], new_kv, memory_grad)


def solution(mesh):
    split = Mesh(mesh.devices.reshape(Y, X, ZL, ZH, C), PIPE + HEAD)
    return jax.shard_map(
        body,
        mesh=split,
        in_specs=(
            P(PIPE, HEAD, None),
            P(None, HEAD, None),
            P(PIPE, None),
            P(),
            P(PIPE, None, HEAD),
            P(PIPE, None, None, HEAD),
            P(PIPE, HEAD, None),
            P(PIPE, None, None, HEAD),
            P(PIPE, None, HEAD),
        ),
        out_specs=(
            P(PIPE, HEAD, None),
            P(PIPE, None, None, HEAD),
            P(PIPE + HEAD, None),
        ),
        check_vma=False,
    )
```

```python
import functools

import jax
import jax.numpy as jnp
from jax import lax
from jax.experimental import pallas as pl
from jax.experimental.pallas import tpu as pltpu
from jax.sharding import Mesh, PartitionSpec as P

TICKS = 2
EPS = 1e-06
PIPE = ("y", "x", "zl")
HEAD = ("zh", "c")
Y, X, ZL, ZH, C = 8, 4, 2, 4, 2
BF, F32 = jnp.bfloat16, jnp.float32


def place(y, x, zl):
    return (y * X + x) * ZL + zl


def norm_into(out, source, scale):
    heads, tokens, width = source.shape
    total = jnp.zeros((tokens, width), F32)
    for h in range(heads):
        wide = source[h].astype(F32)
        total = total + wide * wide
    mean = jnp.sum(total, axis=1, keepdims=True) / (heads * width)
    factor = lax.rsqrt(mean + EPS)
    for h in range(heads):
        wide = source[h].astype(F32)
        out[h] = (wide * factor * scale[:, h * width : (h + 1) * width]).astype(BF)


def project(rows, weight):
    heads, tokens, width = rows.shape
    total = jnp.zeros((tokens, weight.shape[1]), F32)
    for h in range(heads):
        total = total + jnp.dot(
            rows[h], weight[h * width : (h + 1) * width, :], preferred_element_type=F32
        )
    return total.astype(BF)


def attend(query, pair):
    width = query.shape[1]
    scores = lax.dot_general(
        query, pair[:, :width], (((1,), (1,)), ((), ())), preferred_element_type=F32
    )
    scores = scores * width ** (-0.5)
    scores = jnp.exp(scores - jnp.max(scores, axis=-1, keepdims=True))
    probs = (scores / jnp.sum(scores, axis=-1, keepdims=True)).astype(BF)
    return jnp.dot(probs, pair[:, width:], preferred_element_type=F32).astype(BF)


def tick_kernel(tick, half, section, x_hbm, fresh_hbm, gain_hbm, final_hbm, wq_hbm, wkv_hbm, wo_hbm,
                cache_hbm, out_hbm, turned_hbm, x, fresh, turned, gain, final_gain, wq, wkv, wo, pair,
                normed, kv_rows, out, sems):
    heads, tokens, width = x.shape
    here = section[0]
    in_encoder = here < half
    at_half = here == half if tick > 0 else here < 0
    own_pair = jnp.logical_or(in_encoder, at_half)

    def copy(k, source, target):
        return pltpu.make_async_copy(source, target, sems.at[k])

    get_x = copy(0, x_hbm, x)
    get_gain = copy(1, gain_hbm, gain)
    get_wq = copy(2, wq_hbm.at[0], wq)
    get_wkv = copy(3, wkv_hbm.at[0], wkv)
    get_cache = copy(4, cache_hbm.at[0, tick], pair)
    get_wo = copy(5, wo_hbm.at[0], wo)
    get_x.start()
    get_gain.start()
    get_wq.start()
    pl.when(own_pair)(get_wkv.start)
    pl.when(jnp.logical_not(own_pair))(get_cache.start)
    get_wo.start()
    if tick == 0:
        get_fresh = copy(6, fresh_hbm, fresh)
        get_fresh.start()
    get_x.wait()
    get_gain.wait()
    if tick == 0:
        norm_into(normed, x, gain)
        get_fresh.wait()
        for h in range(fresh.shape[0]):
            turned[h] = fresh[h].T
        put_turned = copy(7, turned, turned_hbm)
        put_turned.start()
    else:
        get_fresh = copy(6, fresh_hbm.at[:, 1], fresh)
        get_final = copy(7, final_hbm, final_gain)

        @pl.when(at_half)
        def _():
            get_fresh.start()
            get_final.start()
            get_fresh.wait()
            get_final.wait()
            for h in range(heads):
                turned[h] = fresh[h].T
            norm_into(normed, turned, gain)
            norm_into(kv_rows, x, final_gain)

        @pl.when(jnp.logical_not(at_half))
        def _():
            norm_into(normed, x, gain)

    get_wq.wait()
    query = project(normed, wq)

    @pl.when(in_encoder)
    def _():
        get_wkv.wait()
        pair[:, :width] = project(normed, wkv.at[0])
        pair[:, width:] = project(normed, wkv.at[1])

    if tick > 0:

        @pl.when(at_half)
        def _():
            get_wkv.wait()
            pair[:, :width] = project(kv_rows, wkv.at[0])
            pair[:, width:] = project(kv_rows, wkv.at[1])

    @pl.when(jnp.logical_not(own_pair))
    def _():
        get_cache.wait()

    attn = attend(query, pair)
    get_wo.wait()
    puts = []
    for h in range(heads):
        out[h] = jnp.dot(
            attn, wo[:, h * width : (h + 1) * width], preferred_element_type=F32
        ).astype(BF)
        puts.append(copy(8 + h, out.at[h], out_hbm.at[h]))
        puts[-1].start()
    if tick == 0:
        put_turned.wait()
    for put in puts:
        put.wait()


def first_kernel(half, section, x, fresh, gain, wq, wkv, wo, cache, out, turned, *scratch):
    scratch = scratch[:4] + (None,) + scratch[4:9] + (None,) + scratch[9:]
    tick_kernel(0, half, section, x, fresh, gain, None, wq, wkv, wo, cache, out, turned, *scratch)


def second_kernel(half, section, x, fresh, gain, final, wq, wkv, wo, cache, out, *scratch):
    tick_kernel(1, half, section, x, fresh, gain, final, wq, wkv, wo, cache, out, None, *scratch)


def share_kernel(half, section, grads_hbm, wkv_hbm, out_hbm, grads, wkv, out, sems):
    width = wkv.shape[2]

    @pl.when(section[0] >= half)
    def _():
        get_grads = pltpu.make_async_copy(grads_hbm.at[0], grads, sems.at[0])
        get_wkv = pltpu.make_async_copy(wkv_hbm.at[0], wkv, sems.at[1])
        get_grads.start()
        get_wkv.start()
        get_grads.wait()
        get_wkv.wait()
        rows_by = (((1,), (1,)), ((), ()))
        out[...] = lax.dot_general(
            wkv[0], grads[:, :width], rows_by, preferred_element_type=F32
        ) + lax.dot_general(wkv[1], grads[:, width:], rows_by, preferred_element_type=F32)

    @pl.when(section[0] < half)
    def _():
        out[...] = jnp.zeros_like(out)

    put = pltpu.make_async_copy(out, out_hbm, sems.at[2])
    put.start()
    put.wait()


def memory_kernel(half, section, first_hbm, second_hbm, final_hbm, wkv_hbm, out_hbm, sources, rows,
                  final_gain, wkv, out, sems):
    width = wkv.shape[2]

    def copy(k, source, target):
        return pltpu.make_async_copy(source, target, sems.at[k])

    gets = [
        copy(0, second_hbm, sources.at[1]),
        copy(1, final_hbm, final_gain),
        copy(2, first_hbm.at[:, 0], sources.at[0]),
        copy(3, wkv_hbm.at[0], wkv),
    ]

    @pl.when(section[0] >= half)
    def _():
        for get in gets:
            get.start()
        for get in gets[:3]:
            get.wait()
        for t in range(TICKS):
            norm_into(rows.at[t], sources.at[t], final_gain)
        gets[3].wait()
        for t in range(TICKS):
            out[t, :, :width] = project(rows.at[t], wkv.at[0])
            out[t, :, width:] = project(rows.at[t], wkv.at[1])

    @pl.when(section[0] < half)
    def _():
        out[...] = jnp.zeros_like(out)

    put = copy(4, out, out_hbm.at[0])
    put.start()
    put.wait()


def call(kernel, section, operands, out_shapes, scratch, copies, flops, kind=BF):
    return pl.pallas_call(
        kernel,
        out_shape=[jax.ShapeDtypeStruct(shape, kind) for shape in out_shapes],
        in_specs=[pl.BlockSpec(memory_space=pltpu.SMEM)]
        + [pl.BlockSpec(memory_space=pl.ANY)] * len(operands),
        out_specs=[pl.BlockSpec(memory_space=pl.ANY)] * len(out_shapes),
        scratch_shapes=[pltpu.VMEM(shape, held) for shape, held in scratch]
        + [pltpu.SemaphoreType.DMA((copies,))],
        compiler_params=pltpu.CompilerParams(vmem_limit_bytes=60 * 1024 * 1024),
        cost_estimate=pl.CostEstimate(flops=flops, bytes_accessed=5_000_000, transcendentals=0),
    )(section, *operands)


def spread(block, source, beside):
    y, x, zl = lax.axis_index("y"), lax.axis_index("x"), lax.axis_index("zl")
    sy, sx, sz = source // (X * ZL), source // ZL % X, source % ZL
    held = block
    for to in range(sy + 1, Y):
        sent = lax.ppermute(block, PIPE, [(source, place(to, sx, sz))])
        held = jnp.where(y == to, sent, held)
    column = held
    for to in range(X):
        if to != sx:
            pairs = [(place(k, sx, sz), place(k, to, sz)) for k in range(sy + 1, Y)]
            held = jnp.where(x == to, lax.ppermute(column, PIPE, pairs), held)
    if beside is not None:
        held, beside = lax.optimization_barrier((held, beside))
    pairs = [
        (place(k, to, sz), place(k, to, 1 - sz)) for k in range(sy + 1, Y) for to in range(X)
    ]
    return jnp.where(zl == sz, held, lax.ppermute(held, PIPE, pairs)), beside


def body(stream, fresh, gain, final_gain, w_query, w_kv, w_out, cache_kv, cache_grad):
    pipe_count, heads = Y * X * ZL, ZH * C
    half = pipe_count // 2
    place_here = lax.axis_index(PIPE)
    section = place_here.astype(jnp.int32)[None]
    depth, width = w_kv.shape[2:]
    tokens = stream.shape[2]
    final_scale = final_gain[None]
    rows8 = (heads, tokens, width)
    columns8 = (heads, width, tokens)
    pair_shape = (tokens, 2 * width)
    flops = 2 * tokens * depth * width * 4
    shift = [(i, i + 1) for i in range(pipe_count - 1)]

    def whole(block):
        return lax.all_gather(block, HEAD, axis=0)

    def exchanged(parts):
        return lax.all_to_all(parts, HEAD, 0, 0, tiled=True)

    def summed(parts, current):
        return (current.astype(F32) + jnp.sum(parts.astype(F32), axis=0)).astype(BF)

    weights = (((depth, width), BF), ((2, depth, width), BF), ((width, depth), BF))
    (share,) = call(
        functools.partial(share_kernel, half), section, (cache_grad, w_kv), ((depth, tokens),),
        ((pair_shape, BF), ((2, depth, width), BF), ((depth, tokens), F32)),
        3, flops, F32,
    )
    share, stream = lax.optimization_barrier((share, stream))
    share = lax.psum_scatter(share, "y", scatter_dimension=0, tiled=True)

    fresh_whole = whole(fresh)
    current = stream[0].T
    parts, fresh_rows = call(
        functools.partial(first_kernel, half), section,
        (whole(current), fresh, gain, w_query, w_kv, w_out, cache_kv),
        (rows8, (2, tokens, width)),
        ((rows8, BF), ((2, width, tokens), BF), ((2, tokens, width), BF), ((1, depth), F32))
        + weights + ((pair_shape, BF), (rows8, BF), (rows8, BF)),
        8 + heads, flops,
    )

    output = summed(exchanged(parts), current)
    share, passed = lax.optimization_barrier((share, lax.ppermute(output, PIPE, shift)))
    share = lax.psum_scatter(share, "x", scatter_dimension=0, tiled=True)
    share = share.reshape(ZL * heads, depth // (pipe_count * heads), tokens)
    first_memory, _ = spread(output, half - 1, None)
    entering = output

    current = jnp.where(place_here == 0, fresh_rows[0], passed)
    (parts,) = call(
        functools.partial(second_kernel, half), section,
        (whole(current), fresh_whole, gain, final_scale, w_query, w_kv, w_out, cache_kv),
        (rows8,),
        ((rows8, BF), (columns8, BF), (rows8, BF), ((1, depth), F32), ((1, depth), F32))
        + weights + ((pair_shape, BF), (rows8, BF), (rows8, BF), (rows8, BF)),
        8 + heads, flops,
    )
    current = jnp.where(place_here == half, fresh_rows[1], current)
    parts, first_memory = lax.optimization_barrier((exchanged(parts), first_memory))
    output = summed(parts, current)
    second_memory, share = spread(output, half - 1, share)
    share = lax.all_to_all(share, ("zl",) + HEAD, 0, 0, tiled=True)
    first_memory = whole(jnp.stack([first_memory, entering]))
    passed = lax.ppermute(output, PIPE, shift)
    last = jnp.where(place_here == half, jnp.zeros_like(passed), passed)
    share, second_memory = lax.optimization_barrier((share, whole(second_memory)))
    memory_grad = jnp.sum(share, axis=0)

    (new_kv,) = call(
        functools.partial(memory_kernel, half), section,
        (first_memory, second_memory, final_scale, w_kv),
        ((1, TICKS, tokens, 2 * width),),
        (((TICKS,) + rows8, BF), ((TICKS,) + rows8, BF), ((1, depth), F32),
         ((2, depth, width), BF), ((TICKS,) + pair_shape, BF)),
        5, flops,
    )
    return (last.T[None], new_kv, memory_grad)


def solution(mesh):
    split = Mesh(mesh.devices.reshape(Y, X, ZL, ZH, C), PIPE + HEAD)
    return jax.shard_map(
        body,
        mesh=split,
        in_specs=(
            P(PIPE, HEAD, None),
            P(None, HEAD, None),
            P(PIPE, None),
            P(),
            P(PIPE, None, HEAD),
            P(PIPE, None, None, HEAD),
            P(PIPE, HEAD, None),
            P(PIPE, None, None, HEAD),
            P(PIPE, None, HEAD),
        ),
        out_specs=(
            P(PIPE, HEAD, None),
            P(PIPE, None, None, HEAD),
            P(PIPE + HEAD, None),
        ),
        check_vma=False,
    )
```

```python
import functools

import jax
import jax.numpy as jnp
from jax import lax
from jax.experimental import pallas as pl
from jax.experimental.pallas import tpu as pltpu
from jax.sharding import Mesh, PartitionSpec as P

TICKS = 2
EPS = 1e-06
PIPE = ("y", "x", "zl")
HEAD = ("zh", "c")
Y, X, ZL, ZH, C = 8, 4, 2, 4, 2
BF, F32 = jnp.bfloat16, jnp.float32


def place(y, x, zl):
    return (y * X + x) * ZL + zl


def norm_into(out, source, scale):
    heads, tokens, width = source.shape
    total = jnp.zeros((tokens, width), F32)
    for h in range(heads):
        wide = source[h].astype(F32)
        total = total + wide * wide
    mean = jnp.sum(total, axis=1, keepdims=True) / (heads * width)
    factor = lax.rsqrt(mean + EPS)
    for h in range(heads):
        wide = source[h].astype(F32)
        out[h] = (wide * factor * scale[:, h * width : (h + 1) * width]).astype(BF)


def project(rows, weight):
    heads, tokens, width = rows.shape
    total = jnp.zeros((tokens, weight.shape[1]), F32)
    for h in range(heads):
        total = total + jnp.dot(
            rows[h], weight[h * width : (h + 1) * width, :], preferred_element_type=F32
        )
    return total.astype(BF)


def attend(query, pair):
    width = query.shape[1]
    scores = lax.dot_general(
        query, pair[:, :width], (((1,), (1,)), ((), ())), preferred_element_type=F32
    )
    scores = scores * width ** (-0.5)
    scores = jnp.exp(scores - jnp.max(scores, axis=-1, keepdims=True))
    probs = (scores / jnp.sum(scores, axis=-1, keepdims=True)).astype(BF)
    return jnp.dot(probs, pair[:, width:], preferred_element_type=F32).astype(BF)


def tick_kernel(tick, half, section, x_hbm, fresh_hbm, gain_hbm, final_hbm, wq_hbm, wkv_hbm, wo_hbm,
                cache_hbm, out_hbm, turned_hbm, x, fresh, turned, gain, final_gain, wq, wkv, wo, pair,
                normed, kv_rows, out, sems):
    heads, tokens, width = x.shape
    here = section[0]
    in_encoder = here < half
    at_half = here == half if tick > 0 else here < 0
    own_pair = jnp.logical_or(in_encoder, at_half)

    def copy(k, source, target):
        return pltpu.make_async_copy(source, target, sems.at[k])

    get_x = copy(0, x_hbm, x)
    get_gain = copy(1, gain_hbm, gain)
    get_wq = copy(2, wq_hbm.at[0], wq)
    get_wkv = copy(3, wkv_hbm.at[0], wkv)
    get_cache = copy(4, cache_hbm.at[0, tick], pair)
    get_wo = copy(5, wo_hbm.at[0], wo)
    get_x.start()
    get_gain.start()
    get_wq.start()
    pl.when(own_pair)(get_wkv.start)
    pl.when(jnp.logical_not(own_pair))(get_cache.start)
    get_wo.start()
    if tick == 0:
        get_fresh = copy(6, fresh_hbm, fresh)
        get_fresh.start()
    get_x.wait()
    get_gain.wait()
    if tick == 0:
        norm_into(normed, x, gain)
    else:
        get_fresh = copy(6, fresh_hbm.at[:, 1], fresh)
        get_final = copy(7, final_hbm, final_gain)

        @pl.when(at_half)
        def _():
            get_fresh.start()
            get_final.start()
            get_fresh.wait()
            get_final.wait()
            for h in range(heads):
                turned[h] = fresh[h].T
            norm_into(normed, turned, gain)
            norm_into(kv_rows, x, final_gain)

        @pl.when(jnp.logical_not(at_half))
        def _():
            norm_into(normed, x, gain)

    get_wq.wait()
    query = project(normed, wq)

    @pl.when(in_encoder)
    def _():
        get_wkv.wait()
        pair[:, :width] = project(normed, wkv.at[0])
        pair[:, width:] = project(normed, wkv.at[1])

    if tick > 0:

        @pl.when(at_half)
        def _():
            get_wkv.wait()
            pair[:, :width] = project(kv_rows, wkv.at[0])
            pair[:, width:] = project(kv_rows, wkv.at[1])

    @pl.when(jnp.logical_not(own_pair))
    def _():
        get_cache.wait()

    attn = attend(query, pair)
    get_wo.wait()
    puts = []
    for h in range(heads):
        out[h] = jnp.dot(
            attn, wo[:, h * width : (h + 1) * width], preferred_element_type=F32
        ).astype(BF)
        puts.append(copy(8 + h, out.at[h], out_hbm.at[h % C * ZH + h // C]))
        puts[-1].start()
    if tick == 0:
        get_fresh.wait()
        for h in range(fresh.shape[0]):
            turned[h] = fresh[h].T
        puts.append(copy(7, turned, turned_hbm))
        puts[-1].start()
    for put in puts:
        put.wait()


def first_kernel(half, section, x, fresh, gain, wq, wkv, wo, cache, out, turned, *scratch):
    scratch = scratch[:4] + (None,) + scratch[4:9] + (None,) + scratch[9:]
    tick_kernel(0, half, section, x, fresh, gain, None, wq, wkv, wo, cache, out, turned, *scratch)


def second_kernel(half, section, x, fresh, gain, final, wq, wkv, wo, cache, out, *scratch):
    tick_kernel(1, half, section, x, fresh, gain, final, wq, wkv, wo, cache, out, None, *scratch)


def share_kernel(half, section, grads_hbm, wkv_hbm, out_hbm, grads, wkv, out, sems):
    width = wkv.shape[2]

    @pl.when(section[0] >= half)
    def _():
        get_grads = pltpu.make_async_copy(grads_hbm.at[0], grads, sems.at[0])
        get_wkv = pltpu.make_async_copy(wkv_hbm.at[0], wkv, sems.at[1])
        get_grads.start()
        get_wkv.start()
        get_grads.wait()
        get_wkv.wait()
        rows_by = (((1,), (1,)), ((), ()))
        out[...] = lax.dot_general(
            wkv[0], grads[:, :width], rows_by, preferred_element_type=F32
        ) + lax.dot_general(wkv[1], grads[:, width:], rows_by, preferred_element_type=F32)

    @pl.when(section[0] < half)
    def _():
        out[...] = jnp.zeros_like(out)

    put = pltpu.make_async_copy(out, out_hbm, sems.at[2])
    put.start()
    put.wait()


def memory_kernel(half, section, first_hbm, second_hbm, final_hbm, wkv_hbm, out_hbm, sources, rows,
                  final_gain, wkv, out, sems):
    width = wkv.shape[2]
    tokens = sources.shape[2]

    def copy(k, source, target):
        return pltpu.make_async_copy(source, target, sems.at[k])

    gets = [
        copy(0, second_hbm, sources.at[1]),
        copy(1, final_hbm, final_gain),
        copy(2, first_hbm.at[:, 0], sources.at[0]),
        copy(3, wkv_hbm.at[0], wkv),
    ]

    @pl.when(section[0] >= half)
    def _():
        for get in gets:
            get.start()
        for get in gets[:3]:
            get.wait()
        for t in range(TICKS):
            norm_into(rows.at[:, t * tokens : (t + 1) * tokens], sources.at[t], final_gain)
        gets[3].wait()
        for part in range(2):
            both = project(rows, wkv.at[part])
            for t in range(TICKS):
                out[t, :, part * width : (part + 1) * width] = both[t * tokens : (t + 1) * tokens]

    @pl.when(section[0] < half)
    def _():
        out[...] = jnp.zeros_like(out)

    put = copy(4, out, out_hbm.at[0])
    put.start()
    put.wait()


def call(kernel, section, operands, out_shapes, scratch, copies, flops, kind=BF):
    return pl.pallas_call(
        kernel,
        out_shape=[jax.ShapeDtypeStruct(shape, kind) for shape in out_shapes],
        in_specs=[pl.BlockSpec(memory_space=pltpu.SMEM)]
        + [pl.BlockSpec(memory_space=pl.ANY)] * len(operands),
        out_specs=[pl.BlockSpec(memory_space=pl.ANY)] * len(out_shapes),
        scratch_shapes=[pltpu.VMEM(shape, held) for shape, held in scratch]
        + [pltpu.SemaphoreType.DMA((copies,))],
        compiler_params=pltpu.CompilerParams(vmem_limit_bytes=60 * 1024 * 1024),
        cost_estimate=pl.CostEstimate(flops=flops, bytes_accessed=5_000_000, transcendentals=0),
    )(section, *operands)


def spread(block, source, beside):
    y, x, zl = lax.axis_index("y"), lax.axis_index("x"), lax.axis_index("zl")
    sy, sx, sz = source // (X * ZL), source // ZL % X, source % ZL
    held = block
    for to in range(sy + 1, Y):
        sent = lax.ppermute(block, PIPE, [(source, place(to, sx, sz))])
        held = jnp.where(y == to, sent, held)
    column = held
    for to in range(X):
        if to != sx:
            pairs = [(place(k, sx, sz), place(k, to, sz)) for k in range(sy + 1, Y)]
            held = jnp.where(x == to, lax.ppermute(column, PIPE, pairs), held)
    if beside is not None:
        held, beside = lax.optimization_barrier((held, beside))
    pairs = [
        (place(k, to, sz), place(k, to, 1 - sz)) for k in range(sy + 1, Y) for to in range(X)
    ]
    return jnp.where(zl == sz, held, lax.ppermute(held, PIPE, pairs)), beside


def body(stream, fresh, gain, final_gain, w_query, w_kv, w_out, cache_kv, cache_grad):
    pipe_count, heads = Y * X * ZL, ZH * C
    half = pipe_count // 2
    place_here = lax.axis_index(PIPE)
    section = place_here.astype(jnp.int32)[None]
    depth, width = w_kv.shape[2:]
    tokens = stream.shape[2]
    final_scale = final_gain[None]
    rows8 = (heads, tokens, width)
    columns8 = (heads, width, tokens)
    pair_shape = (tokens, 2 * width)
    flops = 2 * tokens * depth * width * 4
    shift = [(i, i + 1) for i in range(pipe_count - 1)]

    def whole(block):
        return lax.all_gather(block, HEAD, axis=0)

    def exchanged(parts):
        parts = lax.all_to_all(parts.reshape((C, ZH) + parts.shape[1:]), "c", 0, 0, tiled=True)
        parts = jnp.sum(parts.astype(F32), axis=0).astype(BF)
        return lax.all_to_all(parts, "zh", 0, 0, tiled=True)

    def summed(parts, current):
        return (current.astype(F32) + jnp.sum(parts.astype(F32), axis=0)).astype(BF)

    weights = (((depth, width), BF), ((2, depth, width), BF), ((width, depth), BF))
    fresh_whole = whole(fresh)
    current = stream[0].T
    parts, fresh_rows = call(
        functools.partial(first_kernel, half), section,
        (whole(current), fresh, gain, w_query, w_kv, w_out, cache_kv),
        (rows8, (2, tokens, width)),
        ((rows8, BF), ((2, width, tokens), BF), ((2, tokens, width), BF), ((1, depth), F32))
        + weights + ((pair_shape, BF), (rows8, BF), (rows8, BF)),
        8 + heads, flops,
    )

    (share,) = call(
        functools.partial(share_kernel, half), section, (cache_grad, w_kv), ((depth, tokens),),
        ((pair_shape, BF), ((2, depth, width), BF), ((depth, tokens), F32)),
        3, flops, F32,
    )
    share = lax.psum_scatter(share, "y", scatter_dimension=0, tiled=True)
    plane = X * ZL * heads
    share = share.reshape(plane, depth // (pipe_count * heads), tokens)

    output = summed(exchanged(parts), current)
    passed = lax.ppermute(output, PIPE, shift)
    first_memory, _ = spread(output, half - 1, None)
    entering = output

    current = jnp.where(place_here == 0, fresh_rows[0], passed)
    (parts,) = call(
        functools.partial(second_kernel, half), section,
        (whole(current), fresh_whole, gain, final_scale, w_query, w_kv, w_out, cache_kv),
        (rows8,),
        ((rows8, BF), (columns8, BF), (rows8, BF), ((1, depth), F32), ((1, depth), F32))
        + weights + ((pair_shape, BF), (rows8, BF), (rows8, BF), (rows8, BF)),
        8 + heads, flops,
    )
    current = jnp.where(place_here == half, fresh_rows[1], current)
    parts, first_memory = lax.optimization_barrier((exchanged(parts), first_memory))
    output = summed(parts, current)
    second_memory, share = spread(output, half - 1, share)
    share = lax.all_to_all(share, PIPE[1:] + HEAD, 0, 0, tiled=True)
    first_memory = whole(jnp.stack([first_memory, entering]))
    passed = lax.ppermute(output, PIPE, shift)
    last = jnp.where(place_here == half, jnp.zeros_like(passed), passed)
    share, second_memory = lax.optimization_barrier((share, whole(second_memory)))
    memory_grad = jnp.sum(share, axis=0)

    (new_kv,) = call(
        functools.partial(memory_kernel, half), section,
        (first_memory, second_memory, final_scale, w_kv),
        ((1, TICKS, tokens, 2 * width),),
        (((TICKS,) + rows8, BF), ((heads, TICKS * tokens, width), BF), ((1, depth), F32),
         ((2, depth, width), BF), ((TICKS,) + pair_shape, BF)),
        5, flops,
    )
    return (last.T[None], new_kv, memory_grad)


def solution(mesh):
    split = Mesh(mesh.devices.reshape(Y, X, ZL, ZH, C), PIPE + HEAD)
    return jax.shard_map(
        body,
        mesh=split,
        in_specs=(
            P(PIPE, HEAD, None),
            P(None, HEAD, None),
            P(PIPE, None),
            P(),
            P(PIPE, None, HEAD),
            P(PIPE, None, None, HEAD),
            P(PIPE, HEAD, None),
            P(PIPE, None, None, HEAD),
            P(PIPE, None, HEAD),
        ),
        out_specs=(
            P(PIPE, HEAD, None),
            P(PIPE, None, None, HEAD),
            P(PIPE + HEAD, None),
        ),
        check_vma=False,
    )
```

```python
import functools

import jax
import jax.numpy as jnp
from jax import lax
from jax.experimental import pallas as pl
from jax.experimental.pallas import tpu as pltpu
from jax.sharding import Mesh, PartitionSpec as P

TICKS = 2
EPS = 1e-06
PIPE = ("y", "x", "zl")
HEAD = ("zh", "c")
Y, X, ZL, ZH, C = 8, 4, 2, 4, 2
BF, F32 = jnp.bfloat16, jnp.float32


def place(y, x, zl):
    return (y * X + x) * ZL + zl


def norm_into(out, source, scale):
    heads, tokens, width = source.shape
    total = jnp.zeros((tokens, width), F32)
    for h in range(heads):
        wide = source[h].astype(F32)
        total = total + wide * wide
    mean = jnp.sum(total, axis=1, keepdims=True) / (heads * width)
    factor = lax.rsqrt(mean + EPS)
    for h in range(heads):
        wide = source[h].astype(F32)
        out[h] = (wide * factor * scale[:, h * width : (h + 1) * width]).astype(BF)


def project(rows, weight):
    heads, tokens, width = rows.shape
    total = jnp.zeros((tokens, weight.shape[1]), F32)
    for h in range(heads):
        total = total + jnp.dot(
            rows[h], weight[h * width : (h + 1) * width, :], preferred_element_type=F32
        )
    return total.astype(BF)


def attend(query, pair):
    width = query.shape[1]
    scores = lax.dot_general(
        query, pair[:, :width], (((1,), (1,)), ((), ())), preferred_element_type=F32
    )
    scores = scores * width ** (-0.5)
    scores = jnp.exp(scores - jnp.max(scores, axis=-1, keepdims=True))
    probs = (scores / jnp.sum(scores, axis=-1, keepdims=True)).astype(BF)
    return jnp.dot(probs, pair[:, width:], preferred_element_type=F32).astype(BF)


def tick_kernel(tick, half, section, x_hbm, fresh_hbm, gain_hbm, final_hbm, wq_hbm, wkv_hbm, wo_hbm,
                cache_hbm, out_hbm, turned_hbm, x, fresh, turned, gain, final_gain, wq, wkv, wo, pair,
                normed, kv_rows, out, sems):
    heads, tokens, width = x.shape
    here = section[0]
    in_encoder = here < half
    at_half = here == half if tick > 0 else here < 0
    own_pair = jnp.logical_or(in_encoder, at_half)

    def copy(k, source, target):
        return pltpu.make_async_copy(source, target, sems.at[k])

    get_x = copy(0, x_hbm, x)
    get_gain = copy(1, gain_hbm, gain)
    get_wq = copy(2, wq_hbm.at[0], wq)
    get_wkv = copy(3, wkv_hbm.at[0], wkv)
    get_cache = copy(4, cache_hbm.at[0, tick], pair)
    get_wo = copy(5, wo_hbm.at[0], wo)
    get_x.start()
    get_gain.start()
    get_wq.start()
    pl.when(own_pair)(get_wkv.start)
    pl.when(jnp.logical_not(own_pair))(get_cache.start)
    get_wo.start()
    if tick == 0:
        get_fresh = copy(6, fresh_hbm, fresh)
        get_fresh.start()
    get_x.wait()
    get_gain.wait()
    if tick == 0:
        norm_into(normed, x, gain)
    else:
        get_fresh = copy(6, fresh_hbm.at[:, 1], fresh)
        get_final = copy(7, final_hbm, final_gain)

        @pl.when(at_half)
        def _():
            get_fresh.start()
            get_final.start()
            get_fresh.wait()
            get_final.wait()
            for h in range(heads):
                turned[h] = fresh[h].T
            norm_into(normed, turned, gain)
            norm_into(kv_rows, x, final_gain)

        @pl.when(jnp.logical_not(at_half))
        def _():
            norm_into(normed, x, gain)

    get_wq.wait()
    query = project(normed, wq)

    @pl.when(in_encoder)
    def _():
        get_wkv.wait()
        pair[:, :width] = project(normed, wkv.at[0])
        pair[:, width:] = project(normed, wkv.at[1])

    if tick > 0:

        @pl.when(at_half)
        def _():
            get_wkv.wait()
            pair[:, :width] = project(kv_rows, wkv.at[0])
            pair[:, width:] = project(kv_rows, wkv.at[1])

    @pl.when(jnp.logical_not(own_pair))
    def _():
        get_cache.wait()

    attn = attend(query, pair)
    get_wo.wait()
    puts = []
    for h in range(heads):
        out[h] = jnp.dot(
            attn, wo[:, h * width : (h + 1) * width], preferred_element_type=F32
        ).astype(BF)
        puts.append(copy(8 + h, out.at[h], out_hbm.at[h % C * ZH + h // C]))
        puts[-1].start()
    if tick == 0:
        get_fresh.wait()
        for h in range(fresh.shape[0]):
            turned[h] = fresh[h].T
        puts.append(copy(7, turned, turned_hbm))
        puts[-1].start()
    for put in puts:
        put.wait()


def first_kernel(half, section, x, fresh, gain, wq, wkv, wo, cache, out, turned, *scratch):
    scratch = scratch[:4] + (None,) + scratch[4:9] + (None,) + scratch[9:]
    tick_kernel(0, half, section, x, fresh, gain, None, wq, wkv, wo, cache, out, turned, *scratch)


def second_kernel(half, section, x, fresh, gain, final, wq, wkv, wo, cache, out, *scratch):
    tick_kernel(1, half, section, x, fresh, gain, final, wq, wkv, wo, cache, out, None, *scratch)


def share_kernel(half, section, grads_hbm, wkv_hbm, out_hbm, grads, wkv, out, sems):
    width = wkv.shape[2]

    @pl.when(section[0] >= half)
    def _():
        get_grads = pltpu.make_async_copy(grads_hbm.at[0], grads, sems.at[0])
        get_wkv = pltpu.make_async_copy(wkv_hbm.at[0], wkv, sems.at[1])
        get_grads.start()
        get_wkv.start()
        get_grads.wait()
        get_wkv.wait()
        rows_by = (((1,), (1,)), ((), ()))
        out[...] = lax.dot_general(
            wkv[0], grads[:, :width], rows_by, preferred_element_type=F32
        ) + lax.dot_general(wkv[1], grads[:, width:], rows_by, preferred_element_type=F32)

    @pl.when(section[0] < half)
    def _():
        out[...] = jnp.zeros_like(out)

    put = pltpu.make_async_copy(out, out_hbm, sems.at[2])
    put.start()
    put.wait()


def memory_kernel(half, section, first_hbm, second_hbm, final_hbm, wkv_hbm, out_hbm, sources, rows,
                  final_gain, wkv, out, sems):
    width = wkv.shape[2]
    tokens = sources.shape[2]

    def copy(k, source, target):
        return pltpu.make_async_copy(source, target, sems.at[k])

    gets = [
        copy(0, second_hbm, sources.at[1]),
        copy(1, final_hbm, final_gain),
        copy(2, first_hbm.at[:, 0], sources.at[0]),
        copy(3, wkv_hbm.at[0], wkv),
    ]

    @pl.when(section[0] >= half)
    def _():
        for get in gets:
            get.start()
        for get in gets[:3]:
            get.wait()
        for t in range(TICKS):
            norm_into(rows.at[:, t * tokens : (t + 1) * tokens], sources.at[t], final_gain)
        gets[3].wait()
        for part in range(2):
            both = project(rows, wkv.at[part])
            for t in range(TICKS):
                out[t, :, part * width : (part + 1) * width] = both[t * tokens : (t + 1) * tokens]

    @pl.when(section[0] < half)
    def _():
        out[...] = jnp.zeros_like(out)

    put = copy(4, out, out_hbm.at[0])
    put.start()
    put.wait()


def call(kernel, section, operands, out_shapes, scratch, copies, flops, kind=BF):
    return pl.pallas_call(
        kernel,
        out_shape=[jax.ShapeDtypeStruct(shape, kind) for shape in out_shapes],
        in_specs=[pl.BlockSpec(memory_space=pltpu.SMEM)]
        + [pl.BlockSpec(memory_space=pl.ANY)] * len(operands),
        out_specs=[pl.BlockSpec(memory_space=pl.ANY)] * len(out_shapes),
        scratch_shapes=[pltpu.VMEM(shape, held) for shape, held in scratch]
        + [pltpu.SemaphoreType.DMA((copies,))],
        compiler_params=pltpu.CompilerParams(vmem_limit_bytes=60 * 1024 * 1024),
        cost_estimate=pl.CostEstimate(flops=flops, bytes_accessed=5_000_000, transcendentals=0),
    )(section, *operands)


def spread(block, source, beside):
    y, x, zl = lax.axis_index("y"), lax.axis_index("x"), lax.axis_index("zl")
    sy, sx, sz = source // (X * ZL), source // ZL % X, source % ZL
    held = block
    for to in range(sy + 1, Y):
        sent = lax.ppermute(block, PIPE, [(source, place(to, sx, sz))])
        held = jnp.where(y == to, sent, held)
    if beside is not None:
        held, beside = lax.optimization_barrier((held, beside))
    column = held
    for to in range(X):
        if to != sx:
            pairs = [(place(k, sx, sz), place(k, to, sz)) for k in range(sy + 1, Y)]
            held = jnp.where(x == to, lax.ppermute(column, PIPE, pairs), held)
    pairs = [
        (place(k, to, sz), place(k, to, 1 - sz)) for k in range(sy + 1, Y) for to in range(X)
    ]
    return jnp.where(zl == sz, held, lax.ppermute(held, PIPE, pairs)), beside


def body(stream, fresh, gain, final_gain, w_query, w_kv, w_out, cache_kv, cache_grad):
    pipe_count, heads = Y * X * ZL, ZH * C
    half = pipe_count // 2
    place_here = lax.axis_index(PIPE)
    section = place_here.astype(jnp.int32)[None]
    depth, width = w_kv.shape[2:]
    tokens = stream.shape[2]
    final_scale = final_gain[None]
    rows8 = (heads, tokens, width)
    columns8 = (heads, width, tokens)
    pair_shape = (tokens, 2 * width)
    flops = 2 * tokens * depth * width * 4
    shift = [(i, i + 1) for i in range(pipe_count - 1)]

    def whole(block):
        return lax.all_gather(block, HEAD, axis=0)

    def exchanged(parts):
        parts = lax.all_to_all(parts.reshape((C, ZH) + parts.shape[1:]), "c", 0, 0, tiled=True)
        parts = jnp.sum(parts.astype(F32), axis=0).astype(BF)
        return lax.all_to_all(parts, "zh", 0, 0, tiled=True)

    def summed(parts, current):
        return (current.astype(F32) + jnp.sum(parts.astype(F32), axis=0)).astype(BF)

    weights = (((depth, width), BF), ((2, depth, width), BF), ((width, depth), BF))
    fresh_whole = whole(fresh)
    current = stream[0].T
    parts, fresh_rows = call(
        functools.partial(first_kernel, half), section,
        (whole(current), fresh, gain, w_query, w_kv, w_out, cache_kv),
        (rows8, (2, tokens, width)),
        ((rows8, BF), ((2, width, tokens), BF), ((2, tokens, width), BF), ((1, depth), F32))
        + weights + ((pair_shape, BF), (rows8, BF), (rows8, BF)),
        8 + heads, flops,
    )

    (share,) = call(
        functools.partial(share_kernel, half), section, (cache_grad, w_kv), ((depth, tokens),),
        ((pair_shape, BF), ((2, depth, width), BF), ((depth, tokens), F32)),
        3, flops, F32,
    )
    share = lax.psum_scatter(share, "y", scatter_dimension=0, tiled=True)
    plane = X * ZL * heads
    share = share.reshape(plane, depth // (pipe_count * heads), tokens)

    output = summed(exchanged(parts), current)
    passed = lax.ppermute(output, PIPE, shift)
    first_memory, _ = spread(output, half - 1, None)
    entering = output

    current = jnp.where(place_here == 0, fresh_rows[0], passed)
    (parts,) = call(
        functools.partial(second_kernel, half), section,
        (whole(current), fresh_whole, gain, final_scale, w_query, w_kv, w_out, cache_kv),
        (rows8,),
        ((rows8, BF), (columns8, BF), (rows8, BF), ((1, depth), F32), ((1, depth), F32))
        + weights + ((pair_shape, BF), (rows8, BF), (rows8, BF), (rows8, BF)),
        8 + heads, flops,
    )
    current = jnp.where(place_here == half, fresh_rows[1], current)
    parts, first_memory = lax.optimization_barrier((exchanged(parts), first_memory))
    output = summed(parts, current)
    output, share = lax.optimization_barrier((output, share))
    share = lax.all_to_all(share, PIPE[1:] + HEAD, 0, 0, tiled=True)
    second_memory, share = spread(output, half - 1, share)
    first_memory = whole(jnp.stack([first_memory, entering]))
    passed = lax.ppermute(output, PIPE, shift)
    last = jnp.where(place_here == half, jnp.zeros_like(passed), passed)
    second_memory = whole(second_memory)
    memory_grad = jnp.sum(share, axis=0)

    (new_kv,) = call(
        functools.partial(memory_kernel, half), section,
        (first_memory, second_memory, final_scale, w_kv),
        ((1, TICKS, tokens, 2 * width),),
        (((TICKS,) + rows8, BF), ((heads, TICKS * tokens, width), BF), ((1, depth), F32),
         ((2, depth, width), BF), ((TICKS,) + pair_shape, BF)),
        5, flops,
    )
    return (last.T[None], new_kv, memory_grad)


def solution(mesh):
    split = Mesh(mesh.devices.reshape(Y, X, ZL, ZH, C), PIPE + HEAD)
    return jax.shard_map(
        body,
        mesh=split,
        in_specs=(
            P(PIPE, HEAD, None),
            P(None, HEAD, None),
            P(PIPE, None),
            P(),
            P(PIPE, None, HEAD),
            P(PIPE, None, None, HEAD),
            P(PIPE, HEAD, None),
            P(PIPE, None, None, HEAD),
            P(PIPE, None, HEAD),
        ),
        out_specs=(
            P(PIPE, HEAD, None),
            P(PIPE, None, None, HEAD),
            P(PIPE + HEAD, None),
        ),
        check_vma=False,
    )
```

```python
import functools

import jax
import jax.numpy as jnp
from jax import lax
from jax.experimental import pallas as pl
from jax.experimental.pallas import tpu as pltpu
from jax.sharding import Mesh, PartitionSpec as P

TICKS = 2
EPS = 1e-06
PIPE = ("y", "x", "zl")
HEAD = ("zh", "c")
Y, X, ZL, ZH, C = 8, 4, 2, 4, 2
BF, F32 = jnp.bfloat16, jnp.float32


def place(y, x, zl):
    return (y * X + x) * ZL + zl


def norm_into(out, source, scale):
    heads, tokens, width = source.shape
    total = jnp.zeros((tokens, width), F32)
    for h in range(heads):
        wide = source[h].astype(F32)
        total = total + wide * wide
    mean = jnp.sum(total, axis=1, keepdims=True) / (heads * width)
    factor = lax.rsqrt(mean + EPS)
    for h in range(heads):
        wide = source[h].astype(F32)
        out[h] = (wide * factor * scale[:, h * width : (h + 1) * width]).astype(BF)


def project(rows, weight):
    heads, tokens, width = rows.shape
    total = jnp.zeros((tokens, weight.shape[1]), F32)
    for h in range(heads):
        total = total + jnp.dot(
            rows[h], weight[h * width : (h + 1) * width, :], preferred_element_type=F32
        )
    return total.astype(BF)


def attend(query, pair):
    width = query.shape[1]
    scores = lax.dot_general(
        query, pair[:, :width], (((1,), (1,)), ((), ())), preferred_element_type=F32
    )
    scores = scores * width ** (-0.5)
    scores = jnp.exp(scores - jnp.max(scores, axis=-1, keepdims=True))
    probs = (scores / jnp.sum(scores, axis=-1, keepdims=True)).astype(BF)
    return jnp.dot(probs, pair[:, width:], preferred_element_type=F32).astype(BF)


def tick_kernel(tick, half, section, x_hbm, fresh_hbm, gain_hbm, final_hbm, wq_hbm, wkv_hbm, wo_hbm,
                cache_hbm, out_hbm, turned_hbm, x, fresh, turned, gain, final_gain, wq, wkv, wo, pair,
                normed, kv_rows, out, sems):
    heads, tokens, width = x.shape
    here = section[0]
    in_encoder = here < half
    at_half = here == half if tick > 0 else here < 0
    own_pair = jnp.logical_or(in_encoder, at_half)

    def copy(k, source, target):
        return pltpu.make_async_copy(source, target, sems.at[k])

    get_x = copy(0, x_hbm, x)
    get_gain = copy(1, gain_hbm, gain)
    get_wq = copy(2, wq_hbm.at[0], wq)
    get_wkv = copy(3, wkv_hbm.at[0], wkv)
    get_cache = copy(4, cache_hbm.at[0, tick], pair)
    get_wo = copy(5, wo_hbm.at[0], wo)
    get_x.start()
    get_gain.start()
    get_wq.start()
    pl.when(own_pair)(get_wkv.start)
    pl.when(jnp.logical_not(own_pair))(get_cache.start)
    get_wo.start()
    if tick == 0:
        get_fresh = copy(6, fresh_hbm, fresh)
        get_fresh.start()
    get_x.wait()
    get_gain.wait()
    if tick == 0:
        norm_into(normed, x, gain)
    else:
        get_fresh = copy(6, fresh_hbm.at[:, 1], fresh)
        get_final = copy(7, final_hbm, final_gain)

        @pl.when(at_half)
        def _():
            get_fresh.start()
            get_final.start()
            get_fresh.wait()
            get_final.wait()
            for h in range(heads):
                turned[h] = fresh[h].T
            norm_into(normed, turned, gain)
            norm_into(kv_rows, x, final_gain)

        @pl.when(jnp.logical_not(at_half))
        def _():
            norm_into(normed, x, gain)

    get_wq.wait()
    query = project(normed, wq)

    @pl.when(in_encoder)
    def _():
        get_wkv.wait()
        pair[:, :width] = project(normed, wkv.at[0])
        pair[:, width:] = project(normed, wkv.at[1])

    if tick > 0:

        @pl.when(at_half)
        def _():
            get_wkv.wait()
            pair[:, :width] = project(kv_rows, wkv.at[0])
            pair[:, width:] = project(kv_rows, wkv.at[1])

    @pl.when(jnp.logical_not(own_pair))
    def _():
        get_cache.wait()

    attn = attend(query, pair)
    get_wo.wait()
    puts = []
    for h in range(heads):
        out[h] = jnp.dot(
            attn, wo[:, h * width : (h + 1) * width], preferred_element_type=F32
        ).astype(BF)
        puts.append(copy(8 + h, out.at[h], out_hbm.at[h % C * ZH + h // C]))
        puts[-1].start()
    if tick == 0:
        get_fresh.wait()
        for h in range(fresh.shape[0]):
            turned[h] = fresh[h].T
        puts.append(copy(7, turned, turned_hbm))
        puts[-1].start()
    for put in puts:
        put.wait()


def first_kernel(half, section, x, fresh, gain, wq, wkv, wo, cache, out, turned, *scratch):
    scratch = scratch[:4] + (None,) + scratch[4:9] + (None,) + scratch[9:]
    tick_kernel(0, half, section, x, fresh, gain, None, wq, wkv, wo, cache, out, turned, *scratch)


def second_kernel(half, section, x, fresh, gain, final, wq, wkv, wo, cache, out, *scratch):
    tick_kernel(1, half, section, x, fresh, gain, final, wq, wkv, wo, cache, out, None, *scratch)


def share_kernel(half, section, grads_hbm, wkv_hbm, out_hbm, grads, wkv, out, sems):
    width = wkv.shape[2]

    @pl.when(section[0] >= half)
    def _():
        get_grads = pltpu.make_async_copy(grads_hbm.at[0], grads, sems.at[0])
        get_wkv = pltpu.make_async_copy(wkv_hbm.at[0], wkv, sems.at[1])
        get_grads.start()
        get_wkv.start()
        get_grads.wait()
        get_wkv.wait()
        rows_by = (((1,), (1,)), ((), ()))
        out[...] = lax.dot_general(
            wkv[0], grads[:, :width], rows_by, preferred_element_type=F32
        ) + lax.dot_general(wkv[1], grads[:, width:], rows_by, preferred_element_type=F32)

    @pl.when(section[0] < half)
    def _():
        out[...] = jnp.zeros_like(out)

    put = pltpu.make_async_copy(out, out_hbm, sems.at[2])
    put.start()
    put.wait()


def memory_kernel(half, section, first_hbm, second_hbm, final_hbm, wkv_hbm, out_hbm, sources, rows,
                  final_gain, wkv, out, sems):
    width = wkv.shape[2]
    tokens = sources.shape[2]

    def copy(k, source, target):
        return pltpu.make_async_copy(source, target, sems.at[k])

    gets = [
        copy(0, second_hbm, sources.at[1]),
        copy(1, final_hbm, final_gain),
        copy(2, first_hbm.at[:, 0], sources.at[0]),
        copy(3, wkv_hbm.at[0], wkv),
    ]

    @pl.when(section[0] >= half)
    def _():
        for get in gets:
            get.start()
        for get in gets[:3]:
            get.wait()
        for t in range(TICKS):
            norm_into(rows.at[:, t * tokens : (t + 1) * tokens], sources.at[t], final_gain)
        gets[3].wait()
        for part in range(2):
            both = project(rows, wkv.at[part])
            for t in range(TICKS):
                out[t, :, part * width : (part + 1) * width] = both[t * tokens : (t + 1) * tokens]

    @pl.when(section[0] < half)
    def _():
        out[...] = jnp.zeros_like(out)

    put = copy(4, out, out_hbm.at[0])
    put.start()
    put.wait()


def call(kernel, section, operands, out_shapes, scratch, copies, flops, kind=BF):
    return pl.pallas_call(
        kernel,
        out_shape=[jax.ShapeDtypeStruct(shape, kind) for shape in out_shapes],
        in_specs=[pl.BlockSpec(memory_space=pltpu.SMEM)]
        + [pl.BlockSpec(memory_space=pl.ANY)] * len(operands),
        out_specs=[pl.BlockSpec(memory_space=pl.ANY)] * len(out_shapes),
        scratch_shapes=[pltpu.VMEM(shape, held) for shape, held in scratch]
        + [pltpu.SemaphoreType.DMA((copies,))],
        compiler_params=pltpu.CompilerParams(vmem_limit_bytes=60 * 1024 * 1024),
        cost_estimate=pl.CostEstimate(flops=flops, bytes_accessed=5_000_000, transcendentals=0),
    )(section, *operands)


def spread(block, source, beside):
    y, x, zl = lax.axis_index("y"), lax.axis_index("x"), lax.axis_index("zl")
    sy, sx, sz = source // (X * ZL), source // ZL % X, source % ZL
    held = block
    for to in range(sy + 1, Y):
        sent = lax.ppermute(block, PIPE, [(source, place(to, sx, sz))])
        held = jnp.where(y == to, sent, held)
    if beside is not None:
        held, beside = lax.optimization_barrier((held, beside))
    column = held
    for to in range(X):
        if to != sx:
            pairs = [(place(k, sx, sz), place(k, to, sz)) for k in range(sy + 1, Y)]
            held = jnp.where(x == to, lax.ppermute(column, PIPE, pairs), held)
    if beside is not None:
        held, beside = lax.optimization_barrier((held, beside))
    pairs = [
        (place(k, to, sz), place(k, to, 1 - sz)) for k in range(sy + 1, Y) for to in range(X)
    ]
    return jnp.where(zl == sz, held, lax.ppermute(held, PIPE, pairs)), beside


def body(stream, fresh, gain, final_gain, w_query, w_kv, w_out, cache_kv, cache_grad):
    pipe_count, heads = Y * X * ZL, ZH * C
    half = pipe_count // 2
    place_here = lax.axis_index(PIPE)
    section = place_here.astype(jnp.int32)[None]
    depth, width = w_kv.shape[2:]
    tokens = stream.shape[2]
    final_scale = final_gain[None]
    rows8 = (heads, tokens, width)
    columns8 = (heads, width, tokens)
    pair_shape = (tokens, 2 * width)
    flops = 2 * tokens * depth * width * 4
    shift = [(i, i + 1) for i in range(pipe_count - 1)]

    def whole(block):
        return lax.all_gather(block, HEAD, axis=0)

    def exchanged(parts):
        parts = lax.all_to_all(parts.reshape((C, ZH) + parts.shape[1:]), "c", 0, 0, tiled=True)
        parts = jnp.sum(parts.astype(F32), axis=0).astype(BF)
        return lax.all_to_all(parts, "zh", 0, 0, tiled=True)

    def summed(parts, current):
        return (current.astype(F32) + jnp.sum(parts.astype(F32), axis=0)).astype(BF)

    weights = (((depth, width), BF), ((2, depth, width), BF), ((width, depth), BF))
    fresh_whole = whole(fresh)
    current = stream[0].T
    parts, fresh_rows = call(
        functools.partial(first_kernel, half), section,
        (whole(current), fresh, gain, w_query, w_kv, w_out, cache_kv),
        (rows8, (2, tokens, width)),
        ((rows8, BF), ((2, width, tokens), BF), ((2, tokens, width), BF), ((1, depth), F32))
        + weights + ((pair_shape, BF), (rows8, BF), (rows8, BF)),
        8 + heads, flops,
    )

    (share,) = call(
        functools.partial(share_kernel, half), section, (cache_grad, w_kv), ((depth, tokens),),
        ((pair_shape, BF), ((2, depth, width), BF), ((depth, tokens), F32)),
        3, flops, F32,
    )
    share = lax.psum_scatter(share, "y", scatter_dimension=0, tiled=True)
    share = share.reshape(X * ZL, -1, tokens)

    output = summed(exchanged(parts), current)
    passed = lax.ppermute(output, PIPE, shift)
    first_memory, _ = spread(output, half - 1, None)
    entering = output

    current = jnp.where(place_here == 0, fresh_rows[0], passed)
    (parts,) = call(
        functools.partial(second_kernel, half), section,
        (whole(current), fresh_whole, gain, final_scale, w_query, w_kv, w_out, cache_kv),
        (rows8,),
        ((rows8, BF), (columns8, BF), (rows8, BF), ((1, depth), F32), ((1, depth), F32))
        + weights + ((pair_shape, BF), (rows8, BF), (rows8, BF), (rows8, BF)),
        8 + heads, flops,
    )
    current = jnp.where(place_here == half, fresh_rows[1], current)
    parts, first_memory = lax.optimization_barrier((exchanged(parts), first_memory))
    output = summed(parts, current)
    output, share = lax.optimization_barrier((output, share))
    share = lax.all_to_all(share, ("x", "zl"), 0, 0, tiled=True)
    share = jnp.sum(share, axis=0).reshape(heads, -1, tokens)
    second_memory, share = spread(output, half - 1, share)
    share = lax.all_to_all(share, HEAD, 0, 0, tiled=True)
    first_memory = whole(jnp.stack([first_memory, entering]))
    passed = lax.ppermute(output, PIPE, shift)
    last = jnp.where(place_here == half, jnp.zeros_like(passed), passed)
    share, second_memory = lax.optimization_barrier((share, whole(second_memory)))
    memory_grad = jnp.sum(share, axis=0)

    (new_kv,) = call(
        functools.partial(memory_kernel, half), section,
        (first_memory, second_memory, final_scale, w_kv),
        ((1, TICKS, tokens, 2 * width),),
        (((TICKS,) + rows8, BF), ((heads, TICKS * tokens, width), BF), ((1, depth), F32),
         ((2, depth, width), BF), ((TICKS,) + pair_shape, BF)),
        5, flops,
    )
    return (last.T[None], new_kv, memory_grad)


def solution(mesh):
    split = Mesh(mesh.devices.reshape(Y, X, ZL, ZH, C), PIPE + HEAD)
    return jax.shard_map(
        body,
        mesh=split,
        in_specs=(
            P(PIPE, HEAD, None),
            P(None, HEAD, None),
            P(PIPE, None),
            P(),
            P(PIPE, None, HEAD),
            P(PIPE, None, None, HEAD),
            P(PIPE, HEAD, None),
            P(PIPE, None, None, HEAD),
            P(PIPE, None, HEAD),
        ),
        out_specs=(
            P(PIPE, HEAD, None),
            P(PIPE, None, None, HEAD),
            P(PIPE + HEAD, None),
        ),
        check_vma=False,
    )
```

```python
import functools

import jax
import jax.numpy as jnp
from jax import lax
from jax.experimental import pallas as pl
from jax.experimental.pallas import tpu as pltpu
from jax.sharding import Mesh, PartitionSpec as P

TICKS = 2
EPS = 1e-06
PIPE = ("y", "x", "zl")
HEAD = ("zh", "c")
Y, X, ZL, ZH, C = 8, 4, 2, 4, 2
BF, F32 = jnp.bfloat16, jnp.float32


def place(y, x, zl):
    return (y * X + x) * ZL + zl


def norm_into(out, source, scale):
    heads, tokens, width = source.shape
    total = jnp.zeros((tokens, width), F32)
    for h in range(heads):
        wide = source[h].astype(F32)
        total = total + wide * wide
    mean = jnp.sum(total, axis=1, keepdims=True) / (heads * width)
    factor = lax.rsqrt(mean + EPS)
    for h in range(heads):
        wide = source[h].astype(F32)
        out[h] = (wide * factor * scale[:, h * width : (h + 1) * width]).astype(BF)


def project(rows, weight):
    heads, tokens, width = rows.shape
    total = jnp.zeros((tokens, weight.shape[1]), F32)
    for h in range(heads):
        total = total + jnp.dot(
            rows[h], weight[h * width : (h + 1) * width, :], preferred_element_type=F32
        )
    return total.astype(BF)


def attend(query, pair):
    width = query.shape[1]
    scores = lax.dot_general(
        query, pair[:, :width], (((1,), (1,)), ((), ())), preferred_element_type=F32
    )
    scores = scores * width ** (-0.5)
    scores = jnp.exp(scores - jnp.max(scores, axis=-1, keepdims=True))
    probs = (scores / jnp.sum(scores, axis=-1, keepdims=True)).astype(BF)
    return jnp.dot(probs, pair[:, width:], preferred_element_type=F32).astype(BF)


def tick_kernel(tick, half, section, x_hbm, fresh_hbm, gain_hbm, final_hbm, wq_hbm, wkv_hbm, wo_hbm,
                cache_hbm, out_hbm, turned_hbm, x, fresh, turned, gain, final_gain, wq, wkv, wo, pair,
                normed, kv_rows, out, sems):
    heads, tokens, width = x.shape
    here = section[0]
    in_encoder = here < half
    at_half = here == half if tick > 0 else here < 0
    own_pair = jnp.logical_or(in_encoder, at_half)

    def copy(k, source, target):
        return pltpu.make_async_copy(source, target, sems.at[k])

    get_x = copy(0, x_hbm, x)
    get_gain = copy(1, gain_hbm, gain)
    get_wq = copy(2, wq_hbm.at[0], wq)
    get_wkv = copy(3, wkv_hbm.at[0], wkv)
    get_cache = copy(4, cache_hbm.at[0, tick], pair)
    get_wo = copy(5, wo_hbm.at[0], wo)
    get_x.start()
    get_gain.start()
    get_wq.start()
    pl.when(own_pair)(get_wkv.start)
    pl.when(jnp.logical_not(own_pair))(get_cache.start)
    get_wo.start()
    if tick == 0:
        get_fresh = copy(6, fresh_hbm, fresh)
        get_fresh.start()
    get_x.wait()
    get_gain.wait()
    if tick == 0:
        norm_into(normed, x, gain)
    else:
        get_fresh = copy(6, fresh_hbm.at[:, 1], fresh)
        get_final = copy(7, final_hbm, final_gain)

        @pl.when(at_half)
        def _():
            get_fresh.start()
            get_final.start()
            get_fresh.wait()
            get_final.wait()
            for h in range(heads):
                turned[h] = fresh[h].T
            norm_into(normed, turned, gain)
            norm_into(kv_rows, x, final_gain)

        @pl.when(jnp.logical_not(at_half))
        def _():
            norm_into(normed, x, gain)

    get_wq.wait()
    query = project(normed, wq)

    @pl.when(in_encoder)
    def _():
        get_wkv.wait()
        pair[:, :width] = project(normed, wkv.at[0])
        pair[:, width:] = project(normed, wkv.at[1])

    if tick > 0:

        @pl.when(at_half)
        def _():
            get_wkv.wait()
            pair[:, :width] = project(kv_rows, wkv.at[0])
            pair[:, width:] = project(kv_rows, wkv.at[1])

    @pl.when(jnp.logical_not(own_pair))
    def _():
        get_cache.wait()

    attn = attend(query, pair)
    get_wo.wait()
    puts = []
    for h in range(heads):
        out[h] = jnp.dot(
            attn, wo[:, h * width : (h + 1) * width], preferred_element_type=F32
        ).astype(BF)
        puts.append(copy(8 + h, out.at[h], out_hbm.at[h]))
        puts[-1].start()
    if tick == 0:
        get_fresh.wait()
        for h in range(fresh.shape[0]):
            turned[h] = fresh[h].T
        puts.append(copy(7, turned, turned_hbm))
        puts[-1].start()
    for put in puts:
        put.wait()


def first_kernel(half, section, x, fresh, gain, wq, wkv, wo, cache, out, turned, *scratch):
    scratch = scratch[:4] + (None,) + scratch[4:9] + (None,) + scratch[9:]
    tick_kernel(0, half, section, x, fresh, gain, None, wq, wkv, wo, cache, out, turned, *scratch)


def second_kernel(half, section, x, fresh, gain, final, wq, wkv, wo, cache, out, *scratch):
    tick_kernel(1, half, section, x, fresh, gain, final, wq, wkv, wo, cache, out, None, *scratch)


def share_kernel(half, section, grads_hbm, wkv_hbm, out_hbm, grads, wkv, out, sems):
    width = wkv.shape[2]

    @pl.when(section[0] >= half)
    def _():
        get_grads = pltpu.make_async_copy(grads_hbm.at[0], grads, sems.at[0])
        get_wkv = pltpu.make_async_copy(wkv_hbm.at[0], wkv, sems.at[1])
        get_grads.start()
        get_wkv.start()
        get_grads.wait()
        get_wkv.wait()
        rows_by = (((1,), (1,)), ((), ()))
        out[...] = lax.dot_general(
            wkv[0], grads[:, :width], rows_by, preferred_element_type=F32
        ) + lax.dot_general(wkv[1], grads[:, width:], rows_by, preferred_element_type=F32)

    @pl.when(section[0] < half)
    def _():
        out[...] = jnp.zeros_like(out)

    put = pltpu.make_async_copy(out, out_hbm, sems.at[2])
    put.start()
    put.wait()


def last_kernel(half, section, first_hbm, second_hbm, final_hbm, wkv_hbm, passed_hbm, shares_hbm,
                out_hbm, stream_hbm, grad_hbm, sources, rows, final_gain, wkv, passed, shares, out,
                stream, grad, sems):
    width = wkv.shape[2]
    tokens = sources.shape[2]

    def copy(k, source, target):
        return pltpu.make_async_copy(source, target, sems.at[k])

    gets = [
        copy(0, second_hbm, sources.at[1]),
        copy(1, final_hbm, final_gain),
        copy(2, first_hbm.at[:, 0], sources.at[0]),
        copy(3, wkv_hbm.at[0], wkv),
    ]
    get_passed = copy(4, passed_hbm, passed)
    get_shares = copy(5, shares_hbm, shares)

    @pl.when(section[0] >= half)
    def _():
        for get in gets:
            get.start()

    get_passed.start()
    get_shares.start()
    get_passed.wait()
    turned = passed[...].T
    stream[...] = jnp.where(section[0] == half, jnp.zeros_like(turned), turned)
    put_stream = copy(6, stream, stream_hbm.at[0])
    put_stream.start()
    get_shares.wait()
    grad[...] = jnp.sum(shares[...], axis=0)
    put_grad = copy(7, grad, grad_hbm)
    put_grad.start()

    @pl.when(section[0] >= half)
    def _():
        for get in gets[:3]:
            get.wait()
        for t in range(TICKS):
            norm_into(rows.at[:, t * tokens : (t + 1) * tokens], sources.at[t], final_gain)
        gets[3].wait()
        for part in range(2):
            both = project(rows, wkv.at[part])
            for t in range(TICKS):
                out[t, :, part * width : (part + 1) * width] = both[t * tokens : (t + 1) * tokens]

    @pl.when(section[0] < half)
    def _():
        out[...] = jnp.zeros_like(out)

    put = copy(8, out, out_hbm.at[0])
    put.start()
    put_stream.wait()
    put_grad.wait()
    put.wait()


def call(kernel, section, operands, out_shapes, scratch, copies, flops, kinds=None):
    return pl.pallas_call(
        kernel,
        out_shape=[
            jax.ShapeDtypeStruct(shape, kind)
            for shape, kind in zip(out_shapes, kinds or [BF] * len(out_shapes))
        ],
        in_specs=[pl.BlockSpec(memory_space=pltpu.SMEM)]
        + [pl.BlockSpec(memory_space=pl.ANY)] * len(operands),
        out_specs=[pl.BlockSpec(memory_space=pl.ANY)] * len(out_shapes),
        scratch_shapes=[pltpu.VMEM(shape, held) for shape, held in scratch]
        + [pltpu.SemaphoreType.DMA((copies,))],
        compiler_params=pltpu.CompilerParams(vmem_limit_bytes=60 * 1024 * 1024),
        cost_estimate=pl.CostEstimate(flops=flops, bytes_accessed=5_000_000, transcendentals=0),
    )(section, *operands)


def spread(block, source, beside):
    y, x, zl = lax.axis_index("y"), lax.axis_index("x"), lax.axis_index("zl")
    sy, sx, sz = source // (X * ZL), source // ZL % X, source % ZL
    held = block
    for to in range(sy + 1, Y):
        sent = lax.ppermute(block, PIPE, [(source, place(to, sx, sz))])
        held = jnp.where(y == to, sent, held)
    column = held
    for to in range(X):
        if to != sx:
            pairs = [(place(k, sx, sz), place(k, to, sz)) for k in range(sy + 1, Y)]
            held = jnp.where(x == to, lax.ppermute(column, PIPE, pairs), held)
    if beside is not None:
        held, beside = lax.optimization_barrier((held, beside))
    pairs = [
        (place(k, to, sz), place(k, to, 1 - sz)) for k in range(sy + 1, Y) for to in range(X)
    ]
    return jnp.where(zl == sz, held, lax.ppermute(held, PIPE, pairs)), beside


def body(stream, fresh, gain, final_gain, w_query, w_kv, w_out, cache_kv, cache_grad):
    pipe_count, heads = Y * X * ZL, ZH * C
    half = pipe_count // 2
    place_here = lax.axis_index(PIPE)
    section = place_here.astype(jnp.int32)[None]
    depth, width = w_kv.shape[2:]
    tokens = stream.shape[2]
    final_scale = final_gain[None]
    rows8 = (heads, tokens, width)
    columns8 = (heads, width, tokens)
    pair_shape = (tokens, 2 * width)
    flops = 2 * tokens * depth * width * 4
    shift = [(i, i + 1) for i in range(pipe_count - 1)]

    def whole(block):
        return lax.all_gather(block, HEAD, axis=0)

    def exchanged(parts):
        return lax.all_to_all(parts, HEAD, 0, 0, tiled=True)

    def summed(parts, current):
        return (current.astype(F32) + jnp.sum(parts.astype(F32), axis=0)).astype(BF)

    weights = (((depth, width), BF), ((2, depth, width), BF), ((width, depth), BF))
    fresh_whole = whole(fresh)
    current = stream[0].T
    parts, fresh_rows = call(
        functools.partial(first_kernel, half), section,
        (whole(current), fresh, gain, w_query, w_kv, w_out, cache_kv),
        (rows8, (2, tokens, width)),
        ((rows8, BF), ((2, width, tokens), BF), ((2, tokens, width), BF), ((1, depth), F32))
        + weights + ((pair_shape, BF), (rows8, BF), (rows8, BF)),
        8 + heads, flops,
    )

    (share,) = call(
        functools.partial(share_kernel, half), section, (cache_grad, w_kv), ((depth, tokens),),
        ((pair_shape, BF), ((2, depth, width), BF), ((depth, tokens), F32)),
        3, flops, (F32,),
    )
    share = lax.psum_scatter(share, "y", scatter_dimension=0, tiled=True)
    plane = X * ZL * heads
    share = share.reshape(plane, depth // (pipe_count * heads), tokens)

    output = summed(exchanged(parts), current)
    passed = lax.ppermute(output, PIPE, shift)
    first_memory, _ = spread(output, half - 1, None)
    entering = output

    current = jnp.where(place_here == 0, fresh_rows[0], passed)
    (parts,) = call(
        functools.partial(second_kernel, half), section,
        (whole(current), fresh_whole, gain, final_scale, w_query, w_kv, w_out, cache_kv),
        (rows8,),
        ((rows8, BF), (columns8, BF), (rows8, BF), ((1, depth), F32), ((1, depth), F32))
        + weights + ((pair_shape, BF), (rows8, BF), (rows8, BF), (rows8, BF)),
        8 + heads, flops,
    )
    current = jnp.where(place_here == half, fresh_rows[1], current)
    parts, first_memory = lax.optimization_barrier((exchanged(parts), first_memory))
    output = summed(parts, current)
    second_memory, share = spread(output, half - 1, share)
    share = lax.all_to_all(share, PIPE[1:] + HEAD, 0, 0, tiled=True)
    first_memory = whole(jnp.stack([first_memory, entering]))
    passed = lax.ppermute(output, PIPE, shift)
    share, second_memory = lax.optimization_barrier((share, whole(second_memory)))
    each = share.shape[1]
    new_kv, last, memory_grad = call(
        functools.partial(last_kernel, half), section,
        (first_memory, second_memory, final_scale, w_kv, passed, share),
        ((1, TICKS, tokens, 2 * width), (1, width, tokens), (each, tokens)),
        (((TICKS,) + rows8, BF), ((heads, TICKS * tokens, width), BF), ((1, depth), F32),
         ((2, depth, width), BF), ((tokens, width), BF), (share.shape, F32),
         ((TICKS,) + pair_shape, BF), ((width, tokens), BF), ((each, tokens), F32)),
        9, flops, (BF, BF, F32),
    )
    return (last, new_kv, memory_grad)


def solution(mesh):
    split = Mesh(mesh.devices.reshape(Y, X, ZL, ZH, C), PIPE + HEAD)
    return jax.shard_map(
        body,
        mesh=split,
        in_specs=(
            P(PIPE, HEAD, None),
            P(None, HEAD, None),
            P(PIPE, None),
            P(),
            P(PIPE, None, HEAD),
            P(PIPE, None, None, HEAD),
            P(PIPE, HEAD, None),
            P(PIPE, None, None, HEAD),
            P(PIPE, None, HEAD),
        ),
        out_specs=(
            P(PIPE, HEAD, None),
            P(PIPE, None, None, HEAD),
            P(PIPE + HEAD, None),
        ),
        check_vma=False,
    )
```

```python
import functools

import jax
import jax.numpy as jnp
from jax import lax
from jax.experimental import pallas as pl
from jax.experimental.pallas import tpu as pltpu
from jax.sharding import Mesh, PartitionSpec as P

TICKS = 2
EPS = 1e-06
PIPE = ("y", "x", "zl")
HEAD = ("zh", "c")
Y, X, ZL, ZH, C = 8, 4, 2, 4, 2
BF, F32 = jnp.bfloat16, jnp.float32


def place(y, x, zl):
    return (y * X + x) * ZL + zl


def norm_into(out, source, scale):
    heads, tokens, width = source.shape
    total = jnp.zeros((tokens, width), F32)
    for h in range(heads):
        wide = source[h].astype(F32)
        total = total + wide * wide
    mean = jnp.sum(total, axis=1, keepdims=True) / (heads * width)
    factor = lax.rsqrt(mean + EPS)
    for h in range(heads):
        wide = source[h].astype(F32)
        out[h] = (wide * factor * scale[:, h * width : (h + 1) * width]).astype(BF)


def project(rows, weight):
    heads, tokens, width = rows.shape
    total = jnp.zeros((tokens, weight.shape[1]), F32)
    for h in range(heads):
        total = total + jnp.dot(
            rows[h], weight[h * width : (h + 1) * width, :], preferred_element_type=F32
        )
    return total.astype(BF)


def attend(query, pair):
    width = query.shape[1]
    scores = lax.dot_general(
        query, pair[:, :width], (((1,), (1,)), ((), ())), preferred_element_type=F32
    )
    scores = scores * width ** (-0.5)
    scores = jnp.exp(scores - jnp.max(scores, axis=-1, keepdims=True))
    probs = (scores / jnp.sum(scores, axis=-1, keepdims=True)).astype(BF)
    return jnp.dot(probs, pair[:, width:], preferred_element_type=F32).astype(BF)


def tick_kernel(tick, half, section, x_hbm, fresh_hbm, gain_hbm, final_hbm, wq_hbm, wkv_hbm, wo_hbm,
                cache_hbm, out_hbm, turned_hbm, x, fresh, turned, gain, final_gain, wq, wkv, wo, pair,
                normed, kv_rows, out, sems):
    heads, tokens, width = x.shape
    here = section[0]
    in_encoder = here < half
    at_half = here == half if tick > 0 else here < 0
    own_pair = jnp.logical_or(in_encoder, at_half)

    def copy(k, source, target):
        return pltpu.make_async_copy(source, target, sems.at[k])

    get_x = copy(0, x_hbm, x)
    get_gain = copy(1, gain_hbm, gain)
    get_wq = copy(2, wq_hbm.at[0], wq)
    get_wkv = copy(3, wkv_hbm.at[0], wkv)
    get_cache = copy(4, cache_hbm.at[0, tick], pair)
    get_wo = copy(5, wo_hbm.at[0], wo)
    get_x.start()
    get_gain.start()
    get_wq.start()
    pl.when(own_pair)(get_wkv.start)
    pl.when(jnp.logical_not(own_pair))(get_cache.start)
    get_wo.start()
    if tick == 0:
        get_fresh = copy(6, fresh_hbm, fresh)
        get_fresh.start()
    get_x.wait()
    get_gain.wait()
    if tick == 0:
        norm_into(normed, x, gain)
    else:
        get_fresh = copy(6, fresh_hbm.at[:, 1], fresh)
        get_final = copy(7, final_hbm, final_gain)

        @pl.when(at_half)
        def _():
            get_fresh.start()
            get_final.start()
            get_fresh.wait()
            get_final.wait()
            for h in range(heads):
                turned[h] = fresh[h].T
            norm_into(normed, turned, gain)
            norm_into(kv_rows, x, final_gain)

        @pl.when(jnp.logical_not(at_half))
        def _():
            norm_into(normed, x, gain)

    get_wq.wait()
    query = project(normed, wq)

    @pl.when(in_encoder)
    def _():
        get_wkv.wait()
        pair[:, :width] = project(normed, wkv.at[0])
        pair[:, width:] = project(normed, wkv.at[1])

    if tick > 0:

        @pl.when(at_half)
        def _():
            get_wkv.wait()
            pair[:, :width] = project(kv_rows, wkv.at[0])
            pair[:, width:] = project(kv_rows, wkv.at[1])

    @pl.when(jnp.logical_not(own_pair))
    def _():
        get_cache.wait()

    attn = attend(query, pair)
    get_wo.wait()
    puts = []
    for h in range(heads):
        out[h] = jnp.dot(
            attn, wo[:, h * width : (h + 1) * width], preferred_element_type=F32
        ).astype(BF)
        puts.append(copy(8 + h, out.at[h], out_hbm.at[h]))
        puts[-1].start()
    if tick == 0:
        get_fresh.wait()
        for h in range(fresh.shape[0]):
            turned[h] = fresh[h].T
        puts.append(copy(7, turned, turned_hbm))
        puts[-1].start()
    for put in puts:
        put.wait()


def first_kernel(half, section, x, fresh, gain, wq, wkv, wo, cache, out, turned, *scratch):
    scratch = scratch[:4] + (None,) + scratch[4:9] + (None,) + scratch[9:]
    tick_kernel(0, half, section, x, fresh, gain, None, wq, wkv, wo, cache, out, turned, *scratch)


def second_kernel(half, section, x, fresh, gain, final, wq, wkv, wo, cache, out, *scratch):
    tick_kernel(1, half, section, x, fresh, gain, final, wq, wkv, wo, cache, out, None, *scratch)


def share_kernel(half, section, grads_hbm, wkv_hbm, out_hbm, grads, wkv, out, sems):
    width = wkv.shape[2]

    @pl.when(section[0] >= half)
    def _():
        get_grads = pltpu.make_async_copy(grads_hbm.at[0], grads, sems.at[0])
        get_wkv = pltpu.make_async_copy(wkv_hbm.at[0], wkv, sems.at[1])
        get_grads.start()
        get_wkv.start()
        get_grads.wait()
        get_wkv.wait()
        rows_by = (((1,), (1,)), ((), ()))
        out[...] = lax.dot_general(
            wkv[0], grads[:, :width], rows_by, preferred_element_type=F32
        ) + lax.dot_general(wkv[1], grads[:, width:], rows_by, preferred_element_type=F32)

    @pl.when(section[0] < half)
    def _():
        out[...] = jnp.zeros_like(out)

    put = pltpu.make_async_copy(out, out_hbm, sems.at[2])
    put.start()
    put.wait()


def last_kernel(half, section, first_hbm, second_hbm, final_hbm, wkv_hbm, passed_hbm, shares_hbm,
                out_hbm, stream_hbm, grad_hbm, sources, rows, final_gain, wkv, passed, shares, out,
                stream, grad, sems):
    width = wkv.shape[2]
    tokens = sources.shape[2]

    def copy(k, source, target):
        return pltpu.make_async_copy(source, target, sems.at[k])

    gets = [
        copy(0, second_hbm, sources.at[1]),
        copy(1, final_hbm, final_gain),
        copy(2, first_hbm.at[:, 0], sources.at[0]),
        copy(3, wkv_hbm.at[0], wkv),
    ]
    get_passed = copy(4, passed_hbm, passed)
    get_shares = copy(5, shares_hbm, shares)

    @pl.when(section[0] >= half)
    def _():
        for get in gets:
            get.start()

    get_passed.start()
    get_shares.start()
    get_passed.wait()
    turned = passed[...].T
    stream[...] = jnp.where(section[0] == half, jnp.zeros_like(turned), turned)
    put_stream = copy(6, stream, stream_hbm.at[0])
    put_stream.start()
    get_shares.wait()
    grad[...] = jnp.sum(shares[...], axis=0)
    put_grad = copy(7, grad, grad_hbm)
    put_grad.start()

    @pl.when(section[0] >= half)
    def _():
        for get in gets[:3]:
            get.wait()
        for t in range(TICKS):
            norm_into(rows.at[:, t * tokens : (t + 1) * tokens], sources.at[t], final_gain)
        gets[3].wait()
        for part in range(2):
            both = project(rows, wkv.at[part])
            for t in range(TICKS):
                out[t, :, part * width : (part + 1) * width] = both[t * tokens : (t + 1) * tokens]

    @pl.when(section[0] < half)
    def _():
        out[...] = jnp.zeros_like(out)

    put = copy(8, out, out_hbm.at[0])
    put.start()
    put_stream.wait()
    put_grad.wait()
    put.wait()


def call(kernel, section, operands, out_shapes, scratch, copies, flops, kinds=None):
    return pl.pallas_call(
        kernel,
        out_shape=[
            jax.ShapeDtypeStruct(shape, kind)
            for shape, kind in zip(out_shapes, kinds or [BF] * len(out_shapes))
        ],
        in_specs=[pl.BlockSpec(memory_space=pltpu.SMEM)]
        + [pl.BlockSpec(memory_space=pl.ANY)] * len(operands),
        out_specs=[pl.BlockSpec(memory_space=pl.ANY)] * len(out_shapes),
        scratch_shapes=[pltpu.VMEM(shape, held) for shape, held in scratch]
        + [pltpu.SemaphoreType.DMA((copies,))],
        compiler_params=pltpu.CompilerParams(vmem_limit_bytes=60 * 1024 * 1024),
        cost_estimate=pl.CostEstimate(flops=flops, bytes_accessed=5_000_000, transcendentals=0),
    )(section, *operands)


def spread(block, source, beside):
    y, x, zl = lax.axis_index("y"), lax.axis_index("x"), lax.axis_index("zl")
    sy, sx, sz = source // (X * ZL), source // ZL % X, source % ZL
    held = block
    for to in range(sy + 1, Y):
        sent = lax.ppermute(block, PIPE, [(source, place(to, sx, sz))])
        held = jnp.where(y == to, sent, held)
    column = held
    for to in range(X):
        if to != sx:
            pairs = [(place(k, sx, sz), place(k, to, sz)) for k in range(sy + 1, Y)]
            held = jnp.where(x == to, lax.ppermute(column, PIPE, pairs), held)
    if beside is not None:
        held, beside = lax.optimization_barrier((held, beside))
    pairs = [
        (place(k, to, sz), place(k, to, 1 - sz)) for k in range(sy + 1, Y) for to in range(X)
    ]
    return jnp.where(zl == sz, held, lax.ppermute(held, PIPE, pairs)), beside


def body(stream, fresh, gain, final_gain, w_query, w_kv, w_out, cache_kv, cache_grad):
    pipe_count, heads = Y * X * ZL, ZH * C
    half = pipe_count // 2
    place_here = lax.axis_index(PIPE)
    section = place_here.astype(jnp.int32)[None]
    depth, width = w_kv.shape[2:]
    tokens = stream.shape[2]
    final_scale = final_gain[None]
    rows8 = (heads, tokens, width)
    columns8 = (heads, width, tokens)
    pair_shape = (tokens, 2 * width)
    flops = 2 * tokens * depth * width * 4
    shift = [(i, i + 1) for i in range(pipe_count - 1)]

    def whole(block):
        return lax.all_gather(block, HEAD, axis=0)

    def exchanged(parts):
        return lax.all_to_all(parts, HEAD, 0, 0, tiled=True)

    def summed(parts, current):
        return (current.astype(F32) + jnp.sum(parts.astype(F32), axis=0)).astype(BF)

    weights = (((depth, width), BF), ((2, depth, width), BF), ((width, depth), BF))
    fresh_whole = whole(fresh)
    current = stream[0].T
    parts, fresh_rows = call(
        functools.partial(first_kernel, half), section,
        (whole(current), fresh, gain, w_query, w_kv, w_out, cache_kv),
        (rows8, (2, tokens, width)),
        ((rows8, BF), ((2, width, tokens), BF), ((2, tokens, width), BF), ((1, depth), F32))
        + weights + ((pair_shape, BF), (rows8, BF), (rows8, BF)),
        8 + heads, flops,
    )

    (share,) = call(
        functools.partial(share_kernel, half), section, (cache_grad, w_kv), ((depth, tokens),),
        ((pair_shape, BF), ((2, depth, width), BF), ((depth, tokens), F32)),
        3, flops, (F32,),
    )
    share = lax.psum_scatter(share, "y", scatter_dimension=0, tiled=True)
    plane = X * ZL * heads
    share = share.reshape(plane, depth // (pipe_count * heads), tokens)

    output = summed(exchanged(parts), current)
    passed = lax.ppermute(output, PIPE, shift)
    first_memory, _ = spread(output, half - 1, None)
    entering = output

    current = jnp.where(place_here == 0, fresh_rows[0], passed)
    (parts,) = call(
        functools.partial(second_kernel, half), section,
        (whole(current), fresh_whole, gain, final_scale, w_query, w_kv, w_out, cache_kv),
        (rows8,),
        ((rows8, BF), (columns8, BF), (rows8, BF), ((1, depth), F32), ((1, depth), F32))
        + weights + ((pair_shape, BF), (rows8, BF), (rows8, BF), (rows8, BF)),
        8 + heads, flops,
    )
    current = jnp.where(place_here == half, fresh_rows[1], current)
    first_memory = jnp.stack([first_memory, entering])
    parts, _ = lax.optimization_barrier((exchanged(parts), first_memory))
    output = summed(parts, current)
    second_memory, share = spread(output, half - 1, share)
    share = lax.all_to_all(share, PIPE[1:] + HEAD, 0, 0, tiled=True)
    first_memory = whole(first_memory)
    passed = lax.ppermute(output, PIPE, shift)
    share, second_memory = lax.optimization_barrier((share, whole(second_memory)))
    each = share.shape[1]
    new_kv, last, memory_grad = call(
        functools.partial(last_kernel, half), section,
        (first_memory, second_memory, final_scale, w_kv, passed, share),
        ((1, TICKS, tokens, 2 * width), (1, width, tokens), (each, tokens)),
        (((TICKS,) + rows8, BF), ((heads, TICKS * tokens, width), BF), ((1, depth), F32),
         ((2, depth, width), BF), ((tokens, width), BF), (share.shape, F32),
         ((TICKS,) + pair_shape, BF), ((width, tokens), BF), ((each, tokens), F32)),
        9, flops, (BF, BF, F32),
    )
    return (last, new_kv, memory_grad)


def solution(mesh):
    split = Mesh(mesh.devices.reshape(Y, X, ZL, ZH, C), PIPE + HEAD)
    return jax.shard_map(
        body,
        mesh=split,
        in_specs=(
            P(PIPE, HEAD, None),
            P(None, HEAD, None),
            P(PIPE, None),
            P(),
            P(PIPE, None, HEAD),
            P(PIPE, None, None, HEAD),
            P(PIPE, HEAD, None),
            P(PIPE, None, None, HEAD),
            P(PIPE, None, HEAD),
        ),
        out_specs=(
            P(PIPE, HEAD, None),
            P(PIPE, None, None, HEAD),
            P(PIPE + HEAD, None),
        ),
        check_vma=False,
    )
```
